32 devices in a mesh: lat: 16 (over z, x, core), lon: 2 (over y).
Axes of the slice: x: 2, y: 2, z: 4, core: 2. Of those that a mesh axis runs over, the one named last changes fastest.
Arguments:
- clean: float32 [4, 256, 256], P(None, 'lat', 'lon'), may hold values from -6 to 6
- noise: float32 [4, 256, 256], P(None, 'lat', 'lon'), may hold values from -6 to 6
- mean_field: float32 [4, 256, 256], P(None, 'lat', 'lon'), may hold values from -6 to 6
- sigma_index: int32 [1], replicated, may hold values from 0 to 15
- teacher_lift: bfloat16 [128, 8], replicated, may hold values from -2 to 2
- teacher_first: bfloat16 [128, 9, 128], replicated, may hold values from -0.1875 to 0.1875
- teacher_second: bfloat16 [128, 9, 128], replicated, may hold values from -0.1875 to 0.1875
- teacher_proj: bfloat16 [4, 128], replicated, may hold values from -0.5 to 0.5
- student_lift: bfloat16 [128, 8], replicated, may hold values from -2 to 2
- student_first: bfloat16 [128, 9, 128], replicated, may hold values from -0.1875 to 0.1875
- student_second: bfloat16 [128, 9, 128], replicated, may hold values from -0.1875 to 0.1875
- student_proj: bfloat16 [4, 128], replicated, may hold values from -0.5 to 0.5
Outputs:
- target: float32 [4, 256, 256], P(None, 'lat', 'lon')
- update_first: float32 [128, 9, 128], replicated
- update_second: float32 [128, 9, 128], replicated
The draws below stay inside these ranges and needn't reach their ends.
All inputs are finite; a program needn't handle non-finite values.
Results may differ from the reference program's by a relative error of at most 0.0038.
Values may be sent and summed in bfloat16 or wider, within the bound.
A program may use at most 128 MiB of HBM per device.

```python
import jax
import jax.numpy as jnp

V = 4
C = 128
SCHED = 18
NY = 256
NX = 256


def levels(rng, dims, cuts, smallest, top_value):
    def one(position, blocks):
        draws = jax.random.uniform(jax.random.fold_in(jax.random.fold_in(rng, 6), position), (blocks,), jnp.float32, smallest / len(cuts), top_value / len(cuts))
        return jnp.repeat(jnp.exp(draws), dims[position] // blocks).reshape((-1,) + (1,) * (len(dims) - position - 1))

    level = one(*cuts[0])
    for cut in cuts[1:]:
        level = level * one(*cut)
    return level


def scatter_about(key, shape, spread, bound, shards=(), kind=jnp.bfloat16):
    values = jax.random.normal(key, shape, jnp.float32) * spread
    if len(shards) > 0:
        values = levels(key, shape, shards, -0.22, 0.18) * values
    return jnp.clip(values, min=-bound, max=bound).astype(kind)


def setup_inputs(seed: int = 0) -> dict:
    streams_of = jax.random.split(jax.random.key(seed), 13)
    return {
        "clean": scatter_about(streams_of[0], (V, NY, NX), 1.0, 6.0, ((1, 16), (2, 2)), jnp.float32),
        "noise": scatter_about(streams_of[1], (V, NY, NX), 1.0, 6.0, ((1, 16), (2, 2)), jnp.float32),
        "mean_field": scatter_about(streams_of[2], (V, NY, NX), 1.0, 6.0, ((1, 16), (2, 2)), jnp.float32),
        "sigma_index": jax.random.randint(streams_of[3], (1,), 0, SCHED - 2).astype(jnp.int32),
        "teacher_lift": scatter_about(streams_of[4], (C, 2 * V), (2 * V) ** -0.5, 2.0),
        "teacher_first": scatter_about(streams_of[5], (C, 9, C), (9 * C) ** -0.5, 0.1875),
        "teacher_second": scatter_about(streams_of[6], (C, 9, C), (9 * C) ** -0.5, 0.1875),
        "teacher_proj": scatter_about(streams_of[7], (V, C), C ** -0.5, 0.5),
        "student_lift": scatter_about(streams_of[8], (C, 2 * V), (2 * V) ** -0.5, 2.0),
        "student_first": scatter_about(streams_of[9], (C, 9, C), (9 * C) ** -0.5, 0.1875),
        "student_second": scatter_about(streams_of[10], (C, 9, C), (9 * C) ** -0.5, 0.1875),
        "student_proj": scatter_about(streams_of[11], (V, C), C ** -0.5, 0.5),
    }


def plan_sigma(index):
    steps = jnp.arange(SCHED, dtype=jnp.int32)
    ramp = steps.astype(jnp.float32) / (SCHED - 1)
    top = 80.0 ** (1.0 / 7.0)
    bottom = 0.02 ** (1.0 / 7.0)
    table = (top + ramp * (bottom - top)) ** 7.0
    return jnp.sum(jnp.where(steps == index, table, jnp.zeros_like(table)))

def pad_field(field):
    wrapped = jnp.concatenate([field[:, :, -1:], field, field[:, :, :1]], axis=2)
    return jnp.pad(wrapped, ((0, 0), (1, 1), (0, 0)))

def conv_full(padded, kernel):
    rows = padded.shape[1] - 2
    cols = padded.shape[2] - 2
    kernel_f = kernel.astype(jnp.float32)
    padded_f = padded.astype(jnp.float32)
    total = jnp.zeros((kernel.shape[0], rows, cols), jnp.float32)
    for tap in range(9):
        shift_a, shift_b = divmod(tap, 3)
        window = padded_f[:, shift_a:shift_a + rows, shift_b:shift_b + cols]
        total = total + jnp.einsum('oc,chw->ohw', kernel_f[:, tap, :], window)
    return total

def kernel_grad(cotangent, padded):
    rows = cotangent.shape[1]
    cols = cotangent.shape[2]
    cot_f = cotangent.astype(jnp.float32)
    padded_f = padded.astype(jnp.float32)
    taps = []
    for tap in range(9):
        shift_a, shift_b = divmod(tap, 3)
        window = padded_f[:, shift_a:shift_a + rows, shift_b:shift_b + cols]
        taps.append(jnp.einsum('ohw,ihw->oi', cot_f, window))
    return jnp.stack(taps, axis=1)

def flip_kernel(kernel):
    return jnp.transpose(kernel[:, ::-1, :], (2, 1, 0))

def silu_slope(value):
    sig = jax.nn.sigmoid(value)
    return sig * (1.0 + value * (1.0 - sig))

def denoise(state, mean_field, sigma, lift, first, second, proj):
    scale = jnp.sqrt(sigma * sigma + 0.25)
    inputs = jnp.concatenate([state / scale, mean_field], axis=0).astype(jnp.bfloat16)
    hidden0 = jnp.einsum('oc,chw->ohw', lift.astype(jnp.float32), inputs.astype(jnp.float32)).astype(jnp.bfloat16)
    padded0 = pad_field(hidden0)
    before = conv_full(padded0, first)
    hidden1 = jax.nn.silu(before).astype(jnp.bfloat16)
    padded1 = pad_field(hidden1)
    inner = hidden0.astype(jnp.float32) + conv_full(padded1, second)
    gated = jax.nn.silu(inner).astype(jnp.bfloat16)
    field = jnp.einsum('vc,chw->vhw', proj.astype(jnp.float32), gated.astype(jnp.float32))
    denoised = 0.25 / (scale * scale) * state + sigma * 0.5 / scale * field
    return (denoised, (padded0, before, padded1, inner))

def normalize(grad):
    return grad / jnp.sqrt(jnp.mean(grad * grad) + 1e-06)

def reference(clean, noise, mean_field, sigma_index, teacher_lift, teacher_first, teacher_second, teacher_proj, student_lift, student_first, student_second, student_proj):
    start = sigma_index[0]
    sigma0 = plan_sigma(start)
    sigma1 = plan_sigma(start + 1)
    sigma2 = plan_sigma(start + 2)

    def teacher(state, sigma):
        return denoise(state, mean_field, sigma, teacher_lift, teacher_first, teacher_second, teacher_proj)[0]

    def heun(state, low, high):
        slope0 = (state - teacher(state, low)) / low
        guess = state + (high - low) * slope0
        slope1 = (guess - teacher(guess, high)) / high
        return state + (high - low) * 0.5 * (slope0 + slope1)
    state0 = clean + sigma0 * noise
    state2 = heun(heun(state0, sigma0, sigma1), sigma1, sigma2)
    target = state0 - sigma0 * (state2 - state0) / (sigma2 - sigma0)
    denoised, saved = denoise(state0, mean_field, sigma0, student_lift, student_first, student_second, student_proj)
    padded0, before, padded1, inner = saved
    scale = jnp.sqrt(sigma0 * sigma0 + 0.25)
    weight = (sigma0 * sigma0 + 0.25) / (sigma0 * sigma0 * 0.25)
    d_field = (sigma0 * 0.5 / scale * 2.0 * weight * (denoised - target)).astype(jnp.bfloat16)
    d_gated = jnp.einsum('vc,vhw->chw', student_proj.astype(jnp.float32), d_field.astype(jnp.float32))
    d_inner = (d_gated * silu_slope(inner)).astype(jnp.bfloat16)
    grad_second = kernel_grad(d_inner, padded1)
    d_hidden1 = conv_full(pad_field(d_inner), flip_kernel(student_second))
    d_before = (d_hidden1 * silu_slope(before)).astype(jnp.bfloat16)
    grad_first = kernel_grad(d_before, padded0)
    return (target, normalize(grad_first), normalize(grad_second))
```

```python
import functools

import jax
import jax.numpy as jnp
import numpy as np
from jax import lax
from jax.experimental import pallas as pl
from jax.experimental.pallas import tpu as pltpu
from jax.sharding import PartitionSpec as P

SCHED = 18
HALO = 9
SIDE = 16
C = 128
F32 = jnp.float32
BF16 = jnp.bfloat16

LANE = np.arange(128)
LANE_A, LANE_J, LANE_CH = LANE // 32, LANE % 32 // 8, LANE % 8
LANE_SIDE = np.array([1, 0, 1, 0])[LANE_J]


def plan_sigma(index):
    steps = jnp.arange(SCHED, dtype=jnp.int32)
    ramp = steps.astype(F32) / (SCHED - 1)
    top = 80.0 ** (1.0 / 7.0)
    bottom = 0.02 ** (1.0 / 7.0)
    table = (top + ramp * (bottom - top)) ** 7.0
    return jnp.sum(jnp.where(steps == index, table, jnp.zeros_like(table)))


def silu(v):
    u = 0.5 * v
    return u + u * jnp.tanh(u)


def silu_slope(v):
    sig = 0.5 + 0.5 * jnp.tanh(0.5 * v)
    return sig * (1.0 + v * (1.0 - sig))


def kernel(
    rows, pairs, center,
    sc, edge, xin, sel, t_w1, t_w2, t_pr, s_w1, s_w2, s_pr, s_r, s_pt,
    tgt_ref, g2_ref, g1_ref,
    x0, xa, xb, fld, u2, x4, dz4, slope1, slope2, dpre,
):
    total = rows + 2 * HALO
    top = edge[0] == 1
    bottom = edge[1] == 1
    lane = lax.broadcasted_iota(jnp.int32, (1, 1, 128), 2)
    lane_a = lane // 32
    lane_j = lane % 32 // 8
    is_x = lane % 8 < 4

    def zero_edges(ref):
        @pl.when(top)
        def _():
            ref[0:HALO] = jnp.zeros((HALO,) + ref.shape[1:], ref.dtype)

        @pl.when(bottom)
        def _():
            ref[HALO + rows : total] = jnp.zeros((HALO,) + ref.shape[1:], ref.dtype)

    def blocks(first, last, size, body):
        count = -(-(last - first) // size)

        def step(i, carry):
            body(jnp.minimum(first + i * size, last - size))
            return carry

        lax.fori_loop(0, count, step, 0)

    def load_state(r):
        part = xin[pl.ds(r, 2)].reshape(2 * pairs, 16)
        x0[pl.ds(r, 2)] = jnp.dot(
            part, sel[...], precision=lax.Precision.HIGHEST, preferred_element_type=F32
        ).reshape(2, pairs, 128)

    blocks(0, total, 2, load_state)

    def spread(value, ref, r, nb):
        for n in range(nb):
            row = value[n]
            ref[r + n, :, 0:128] = pltpu.roll(row[:, 128:], 1, 0).astype(BF16)
            ref[r + n, :, 128:384] = row.astype(BF16)
            ref[r + n, :, 384:512] = pltpu.roll(row[:, :128], pairs - 1, 0).astype(BF16)

    def conv1(state, q_inv, w1, first, last, nb, save):
        scale = jnp.where(is_x, q_inv, 1.0)

        def body(r):
            xs = state[pl.ds(r - 1, nb + 2)] * scale
            shifted = []
            for n in range(nb + 2):
                row = xs[n]
                back = pltpu.roll(row, 1, 0)
                ahead = pltpu.roll(row, pairs - 1, 0)
                shifted.append(jnp.where(lane_j[0] == 0, back, jnp.where(lane_j[0] == 3, ahead, row)))
            u = jnp.stack(
                [
                    jnp.where(
                        lane_a[0] == 0,
                        shifted[n],
                        jnp.where(lane_a[0] == 1, shifted[n + 1], shifted[n + 2]),
                    )
                    for n in range(nb)
                ]
            ).astype(BF16)
            u2[pl.ds(r, nb)] = u
            flat = u.reshape(nb * pairs, 128)
            pre = jnp.dot(
                jnp.concatenate([flat, flat], axis=1), w1[...], preferred_element_type=F32
            ).reshape(nb, pairs, 256)
            spread(silu(pre), x4, r, nb)
            if save:
                slope1[pl.ds(r, nb)] = silu_slope(pre)

        blocks(first, last, nb, body)
        zero_edges(x4)

    def conv2(w2, pr, first, last, nb, save):
        def body(r):
            lhs = jnp.concatenate(
                [x4[pl.ds(r + a - 1, nb)].reshape(nb * pairs, 512) for a in range(3)]
                + [u2[pl.ds(r, nb)].reshape(nb * pairs, 128)],
                axis=1,
            )
            z = jnp.dot(lhs, w2[...], preferred_element_type=F32)
            g = silu(z).astype(BF16)
            fld[pl.ds(r, nb)] = jnp.dot(g, pr[...], preferred_element_type=F32).reshape(
                nb, pairs, 128
            )
            if save:
                slope2[pl.ds(r, nb)] = silu_slope(z).reshape(nb, pairs, 256)

        blocks(first, last, nb, body)
        zero_edges(fld)

    s0, s1, s2 = sc[0], sc[1], sc[2]
    q_inv = [sc[3], sc[4], sc[5]]
    rest = [sc[6], sc[7], sc[8]]
    keep = [sc[9], sc[10], sc[11]]
    gain = [sc[12], sc[13], sc[14]]
    h0, h1 = sc[15], sc[16]
    h0_a, h0_b, h1_b, h1_c = sc[17], sc[18], sc[19], sc[20]
    back = sc[21]
    pull = sc[22]

    def teacher(state, level, first):
        last = total - first
        conv1(state, q_inv[level], t_w1, first, last, 4, False)
        conv2(t_w2, t_pr, first + 1, last - 1, 6, False)

    def update(dst, first, fn):
        def body(r):
            at = pl.ds(r, 2)
            dst[at] = fn(at)

        blocks(first, total - first, 2, body)

    def euler(src, dst, first, level, ratio):
        cx = jnp.where(is_x, 1.0 + ratio * rest[level], 1.0)
        cf = ratio * gain[level]
        update(dst, first, lambda at: src[at] * cx - fld[at] * cf)

    def correct(src, guess, dst, first, level, ratio):
        cx = jnp.where(is_x, 0.5 + 0.5 * ratio * rest[level], 0.5)
        cf = 0.5 * ratio * gain[level]
        update(dst, first, lambda at: 0.5 * src[at] + guess[at] * cx - fld[at] * cf)

    teacher(x0, 0, 1)
    euler(x0, xa, 2, 0, h0_a)
    teacher(xa, 1, 3)
    correct(x0, xa, xb, 4, 1, h0_b)
    teacher(xb, 1, 5)
    euler(xb, xa, 6, 1, h1_b)
    teacher(xa, 2, 7)
    correct(xb, xa, xb, 8, 2, h1_c)

    def make_target(at):
        start = x0[at]
        return start - (xb[at] - start) * back

    update(xa, 8, make_target)
    tgt_ref[...] = xa[HALO : HALO + rows, 0:center, :]

    conv1(x0, q_inv[0], s_w1, 7, total - 7, 4, True)
    conv2(s_w2, s_pr, 8, total - 8, 6, True)

    def backward(r):
        at = pl.ds(r, 2)
        d_field = jnp.where(
            is_x, pull * (keep[0] * x0[at] + gain[0] * fld[at] - xa[at]), 0.0
        ).astype(BF16)
        d_gated = jnp.dot(
            d_field.reshape(2 * pairs, 128), s_pt[...], preferred_element_type=F32
        ).reshape(2, pairs, 256)
        spread(d_gated * slope2[at], dz4, r, 2)

    blocks(8, total - 8, 2, backward)
    zero_edges(dz4)

    cells = rows * center
    dims = (((0,), (0,)), ((), ()))
    middle = pl.ds(HALO, rows)
    dz = dz4[middle, 0:center, 128:384].reshape(cells, 256)
    for a in range(3):
        near = x4[pl.ds(HALO - 1 + a, rows), 0:center, :].reshape(cells, 512)
        grad = lax.dot_general(dz, near, dims, preferred_element_type=F32)
        g2_ref[:, a * 384 : (a + 1) * 384] = grad[:128, 0:384] + grad[128:, 128:512]

    def conv3(r):
        lhs = jnp.concatenate(
            [dz4[pl.ds(r + a - 1, 4)].reshape(4 * pairs, 512) for a in range(3)], axis=1
        )
        dh = jnp.dot(lhs, s_r[...], preferred_element_type=F32).reshape(4, pairs, 256)
        dpre[pl.ds(r - HALO, 4)] = (dh * slope1[pl.ds(r, 4)]).astype(BF16)

    blocks(HALO, HALO + rows, 4, conv3)
    d_before = dpre[:, 0:center, :].reshape(cells, 256)
    near = u2[middle, 0:center, :].reshape(cells, 128)
    grad = lax.dot_general(d_before, near, dims, preferred_element_type=F32)
    g1_ref[...] = grad[:128] + pltpu.roll(grad[128:], 120, 1)


def pair_weights(taps):
    none = jnp.zeros_like(taps[:, :1])
    even = jnp.concatenate([taps, none], axis=1)
    odd = jnp.concatenate([none, taps], axis=1)
    both = jnp.concatenate([even, odd], axis=3)
    return both.reshape(12 * taps.shape[2], 2 * taps.shape[3])


def second_weights(second, lift):
    taps = second.reshape(C, 3, 3, C).transpose(1, 2, 3, 0)
    lift_t = lift.T
    none = jnp.zeros((8, C), lift.dtype)
    center = jnp.concatenate(
        [
            jnp.zeros((40, 2 * C), lift.dtype),
            jnp.concatenate([lift_t, none], axis=1),
            jnp.concatenate([none, lift_t], axis=1),
            jnp.zeros((72, 2 * C), lift.dtype),
        ],
        axis=0,
    )
    return jnp.concatenate([pair_weights(taps), center], axis=0)


def first_weights(first, lift):
    joined = jnp.einsum("oti,ic->tco", first, lift, preferred_element_type=F32)
    full = pair_weights(joined.reshape(3, 3, 8, C))
    full = jnp.pad(full, ((0, 32), (0, 0)))
    high = lax.reduce_precision(full, 8, 7)
    return jnp.concatenate([high, full - high], axis=0).astype(BF16)


def proj_weights(proj):
    spot = (LANE_CH < 4) & (LANE < 96)
    wide = jnp.where(spot[None, :], proj.T[:, LANE_CH % 4], 0)
    even = jnp.where((LANE_SIDE == 0)[None, :], wide, 0)
    odd = jnp.where((LANE_SIDE == 1)[None, :], wide, 0)
    return jnp.concatenate([even, odd], axis=0).astype(BF16)


def back_weights(proj):
    four = jnp.concatenate([proj, jnp.zeros_like(proj)], axis=0)
    none = jnp.zeros_like(four)
    return jnp.concatenate(
        [
            jnp.zeros((40, 2 * C), proj.dtype),
            jnp.concatenate([four, none], axis=1),
            jnp.concatenate([none, four], axis=1),
            jnp.zeros((72, 2 * C), proj.dtype),
        ],
        axis=0,
    )


def local(
    clean, noise, mean_field, sigma_index,
    teacher_lift, teacher_first, teacher_second, teacher_proj,
    student_lift, student_first, student_second, student_proj,
):
    start = sigma_index[0]
    s0, s1, s2 = plan_sigma(start), plan_sigma(start + 1), plan_sigma(start + 2)
    sig = jnp.stack([s0, s1, s2])
    q2 = sig * sig + 0.25
    q = jnp.sqrt(q2)
    weight = q2[0] / (s0 * s0 * 0.25)
    h0, h1 = s1 - s0, s2 - s1
    scalars = jnp.concatenate(
        [
            sig, 1.0 / q, sig * sig / q2, 0.25 / q2, sig * 0.5 / q,
            jnp.stack(
                [h0, h1, h0 / s0, h0 / s1, h1 / s1, h1 / s2, s0 / (s2 - s0),
                 s0 * 0.5 / q[0] * 2.0 * weight]
            ),
        ]
    )
    rows, cols = clean.shape[1:]
    lat, lon = lax.axis_size("lat"), lax.axis_size("lon")
    me = lax.axis_index("lat")
    edge = jnp.stack([me == 0, me == lat - 1]).astype(jnp.int32)

    cells = jnp.concatenate([clean + s0 * noise, mean_field], axis=0)
    ring = [(i, (i + 1) % lon) for i in range(lon)]
    left = lax.ppermute(cells[:, :, cols - SIDE :], "lon", ring)
    right = lax.ppermute(cells[:, :, :SIDE], "lon", [(b, a) for a, b in ring])
    cells = jnp.concatenate([cells, right, left], axis=2)
    up = [(i, i + 1) for i in range(lat - 1)]
    above = lax.ppermute(cells[:, rows - HALO :], "lat", up)
    below = lax.ppermute(cells[:, :HALO], "lat", [(b, a) for a, b in up])
    cells = jnp.concatenate([above, cells, below], axis=1)
    total, pairs, center = rows + 2 * HALO, (cols + 2 * SIDE) // 2, cols // 2
    xin = cells.reshape(8, total, pairs, 2).transpose(1, 2, 3, 0).reshape(total, pairs, 16)

    sel = (
        (np.arange(16)[:, None] == (LANE_SIDE * 8 + LANE_CH)[None, :]) & (LANE < 96)[None, :]
    ).astype(np.float32)
    back = student_second[:, ::-1, :].reshape(C, 3, 3, C).transpose(1, 2, 0, 3)
    operands = [
        scalars, edge, xin, jnp.asarray(sel),
        first_weights(teacher_first, teacher_lift),
        second_weights(teacher_second, teacher_lift),
        proj_weights(teacher_proj),
        first_weights(student_first, student_lift),
        second_weights(student_second, student_lift),
        proj_weights(student_proj),
        pair_weights(back),
        back_weights(student_proj),
    ]
    vmem = pl.BlockSpec(memory_space=pltpu.VMEM)
    smem = pl.BlockSpec(memory_space=pltpu.SMEM)
    tgt, g2, g1 = pl.pallas_call(
        functools.partial(kernel, rows, pairs, center),
        out_shape=[
            jax.ShapeDtypeStruct((rows, center, 128), F32),
            jax.ShapeDtypeStruct((C, 9 * C), F32),
            jax.ShapeDtypeStruct((C, 128), F32),
        ],
        in_specs=[smem, smem] + [vmem] * 10,
        out_specs=[vmem] * 3,
        scratch_shapes=[pltpu.VMEM((total, pairs, 128), F32)] * 4
        + [
            pltpu.VMEM((total, pairs, 128), BF16),
            pltpu.VMEM((total, pairs, 512), BF16),
            pltpu.VMEM((total, pairs, 512), BF16),
            pltpu.VMEM((total, pairs, 256), F32),
            pltpu.VMEM((total, pairs, 256), F32),
            pltpu.VMEM((rows, pairs, 256), BF16),
        ],
        compiler_params=pltpu.CompilerParams(vmem_limit_bytes=56 * 1024 * 1024),
    )(*operands)
    target = (
        tgt[:, :, 8:24].reshape(rows, center, 2, 8)[..., :4].transpose(3, 0, 1, 2)
    ).reshape(4, rows, cols)
    g2, g1 = lax.psum((g2, g1), ("lat", "lon"))
    spots = g1[:, :96].reshape(C, 3, 4, 8)[:, :, :3].reshape(C, 9, 8)
    grad_first = jnp.einsum(
        "otc,ic->oti", spots, student_lift.astype(F32), precision=lax.Precision.HIGHEST
    )
    update_first = grad_first * lax.rsqrt(jnp.mean(grad_first * grad_first) + 1e-06)
    update_second = g2 * lax.rsqrt(jnp.mean(g2 * g2) + 1e-06)
    return (target, update_first, update_second.reshape(C, 9, C))


def solution(mesh):
    grid = P(None, "lat", "lon")
    return jax.shard_map(
        local,
        mesh=mesh,
        in_specs=(grid, grid, grid) + (P(),) * 9,
        out_specs=(grid, P(), P()),
        check_vma=False,
    )
```

```python
import functools

import jax
import jax.numpy as jnp
import numpy as np
from jax import lax
from jax.experimental import pallas as pl
from jax.experimental.pallas import tpu as pltpu
from jax.sharding import PartitionSpec as P

SCHED = 18
HALO = 9
SIDE = 16
C = 128
F32 = jnp.float32
BF16 = jnp.bfloat16


def scalar_table():
    ramp = np.arange(SCHED, dtype=np.float64) / (SCHED - 1)
    top, bottom = 80.0 ** (1.0 / 7.0), 0.02 ** (1.0 / 7.0)
    sigma = (top + ramp * (bottom - top)) ** 7.0
    rows = []
    for n in range(SCHED - 2):
        sig = sigma[n : n + 3]
        s0, s1, s2 = sig
        q2 = sig * sig + 0.25
        q = np.sqrt(q2)
        lam = q2[0] / (s0 * s0 * 0.25)
        h0, h1 = s1 - s0, s2 - s1
        rows.append(
            [*sig, *(1.0 / q), *(sig * sig / q2), *(0.25 / q2), *(sig * 0.5 / q)]
            + [h0, h1, h0 / s0, h0 / s1, h1 / s1, h1 / s2, s0 / (s2 - s0)]
            + [s0 * 0.5 / q[0] * 2.0 * lam]
        )
    return np.asarray(rows, np.float32)


N_SCALARS = 23
MESH = pl.DeviceIdType.MESH


def halo_kernel(lat_n, lon_n, offsets, table, index, clean, noise, mean, out, send, recv):
    y, x = lax.axis_index("lat"), lax.axis_index("lon")
    partners = []
    for dy in (0, 1, -1):
        for n, dx in enumerate(offsets):
            if dy or dx:
                back = [(-dx - other) % lon_n for other in offsets].index(0)
                partners.append(
                    (lax.rem(y + dy + lat_n, lat_n), lax.rem(x + dx + lon_n, lon_n), 1 - dy, back)
                )
    barrier = pltpu.get_barrier_semaphore()
    for py, px, _, _ in partners:
        pl.semaphore_signal(barrier, inc=1, device_id=(py, px), device_id_type=MESH)
    out[1, 0, 0:4] = clean[...] + table[index[0] * N_SCALARS] * noise[...]
    out[1, 0, 4:8] = mean[...]
    pl.semaphore_wait(barrier, len(partners))
    copies = []
    for k, (py, px, sy, sx) in enumerate(partners):
        copy = pltpu.make_async_remote_copy(
            src_ref=out.at[1, 0],
            dst_ref=out.at[sy, sx],
            send_sem=send.at[k],
            recv_sem=recv.at[k],
            device_id=(py, px),
            device_id_type=MESH,
        )
        copy.start()
        copies.append(copy)
    for copy in copies:
        copy.wait()


def sum_kernel(
    inner, depth, lon_n, chunk, piece,
    part, lift, first_ref, second_ref,
    outgoing, plane_in, held, line_in, line_all, plane_all, send, recv,
):
    y, x = lax.axis_index("lat"), lax.axis_index("lon")
    plane = inner * lon_n
    line = lax.div(y, inner)
    spot = lax.rem(y, inner) * lon_n + x

    def in_plane(step):
        other = lax.rem(spot + step, plane)
        return other, (line * inner + lax.div(other, lon_n), lax.rem(other, lon_n))

    def in_line(step):
        other = lax.rem(line + step, depth)
        return other, (other * inner + lax.rem(y, inner), x)

    barrier = pltpu.get_barrier_semaphore()
    for step in range(1, plane):
        pl.semaphore_signal(barrier, inc=1, device_id=in_plane(step)[1], device_id_type=MESH)
    for step in range(1, depth):
        pl.semaphore_signal(barrier, inc=1, device_id=in_line(step)[1], device_id_type=MESH)
    for n in range(plane):
        outgoing[n] = part[n * chunk : (n + 1) * chunk].astype(BF16)
    pl.semaphore_wait(barrier, plane + depth - 2)

    used = [0]

    def exchange(count, where, source, target):
        copies = []
        for step in range(1, count):
            other, device = where(step)
            k = used[0]
            used[0] += 1
            copy = pltpu.make_async_remote_copy(
                src_ref=source(other),
                dst_ref=target(step),
                send_sem=send.at[k],
                recv_sem=recv.at[k],
                device_id=device,
                device_id_type=MESH,
            )
            copy.start()
            copies.append(copy)
        for copy in copies:
            copy.wait()

    exchange(plane, in_plane, lambda o: outgoing.at[o], lambda step: plane_in.at[step - 1])
    own = part[pl.ds(pl.multiple_of(spot * chunk, 8), chunk)]
    for n in range(plane - 1):
        own = own + plane_in[n].astype(F32)
    for n in range(depth):
        held[n] = own[n * piece : (n + 1) * piece]
    exchange(depth, in_line, lambda o: held.at[o], lambda step: line_in.at[step - 1])
    whole = held[line]
    for n in range(depth - 1):
        whole = whole + line_in[n]
    line_all[line] = whole
    exchange(depth, in_line, lambda o: line_all.at[line], lambda step: line_all.at[line])
    plane_all[spot] = line_all[...].reshape(chunk, 128).astype(BF16)
    exchange(plane, in_plane, lambda o: plane_all.at[spot], lambda step: plane_all.at[spot])

    total = plane_all[...].reshape(plane * chunk, 128).astype(F32)
    size = 1.0 / (9 * C * C)
    second = [total[t * C : (t + 1) * C] for t in range(9)]
    spots = total[9 * C : 10 * C]
    tall = jnp.concatenate([lift[...]] * 16, axis=0)
    group = lax.broadcasted_iota(jnp.int32, (128, 128), 0) // 8
    first = [
        jnp.dot(
            spots,
            jnp.where(group == 4 * (t // 3) + t % 3, tall, 0.0),
            precision=lax.Precision.HIGHEST,
            preferred_element_type=F32,
        )
        for t in range(9)
    ]
    for blocks, ref in ((first, first_ref), (second, second_ref)):
        squares = blocks[0] * blocks[0]
        for t in range(1, 9):
            squares = squares + blocks[t] * blocks[t]
        factor = lax.rsqrt(jnp.sum(squares, keepdims=True) * size + 1e-06)
        for t in range(9):
            ref[:, t, :] = blocks[t] * factor


def silu(v):
    u = 0.5 * v
    return u + u * jnp.tanh(u)


def silu_slope(v):
    sig = 0.5 + 0.5 * jnp.tanh(0.5 * v)
    return sig * (1.0 + v * (1.0 - sig))


def kernel(
    rows, pairs, center,
    table, index, blocks_in, taps, lifts, projs,
    tgt_ref, sum_ref,
    x0, xa, xb, fld, u2, x4, dz4, slope1, slope2, dpre,
    t_w1, t_w2, t_pr, s_w1, s_w2, s_pr, s_r, s_pt, joined, turned,
):
    total = rows + 2 * HALO
    me = lax.axis_index("lat")
    top = me == 0
    bottom = me == lax.axis_size("lat") - 1
    base = index[0] * N_SCALARS
    sc = [table[base + k] for k in range(N_SCALARS)]
    lane = lax.broadcasted_iota(jnp.int32, (1, 1, 128), 2)
    lane_a = lane // 32
    lane_j = lane % 32 // 8
    is_x = lane % 8 < 4

    def zero_edges(ref):
        @pl.when(top)
        def _():
            ref[0:HALO] = jnp.zeros((HALO,) + ref.shape[1:], ref.dtype)

        @pl.when(bottom)
        def _():
            ref[HALO + rows : total] = jnp.zeros((HALO,) + ref.shape[1:], ref.dtype)

    def blocks(first, last, size, body):
        count = -(-(last - first) // size)

        def step(i, carry):
            body(jnp.minimum(first + i * size, last - size))
            return carry

        lax.fori_loop(0, count, step, 0)

    cols = 2 * center
    ch_of = lax.broadcasted_iota(jnp.int32, (8, 128), 0)
    lane_of = lax.broadcasted_iota(jnp.int32, (8, 128), 1)
    sel = jnp.where((lane_of % 8 == ch_of) & (lane_of < 96), 1.0, 0.0).astype(F32)
    odd_lane = (lane_j[0] == 0) | (lane_j[0] == 2)
    last_slot = blocks_in.shape[1] - 1

    def load_rows(slot, source, first, count):
        def step(i, carry):
            def turn(part):
                return lax.dot_general(
                    part, sel, (((0,), (0,)), ((), ())),
                    precision=lax.Precision.HIGHEST, preferred_element_type=F32,
                )

            turned[0:cols] = turn(blocks_in[slot, 0, :, source + i, :])
            turned[cols : cols + SIDE] = turn(blocks_in[slot, 1, :, source + i, :])[:SIDE]
            turned[cols + SIDE : cols + 2 * SIDE] = turn(
                blocks_in[slot, last_slot, :, source + i, :]
            )[cols - SIDE :]
            even = turned[pl.ds(0, pairs, stride=2)]
            odd = turned[pl.ds(1, pairs, stride=2)]
            x0[first + i] = jnp.where(odd_lane, odd, even)
            return carry

        lax.fori_loop(0, count, step, 0)

    load_rows(0, rows - HALO, 0, HALO)
    load_rows(1, 0, HALO, rows)
    load_rows(2, 0, HALO + rows, HALO)
    zero_edges(x0)

    def place(ref, t, block):
        a, b = divmod(t, 3)
        for side in range(2):
            at = (4 * a + b + side) * C
            ref[at : at + C, side * C : (side + 1) * C] = block

    for ref in (t_w2, s_w2, s_r):
        ref[...] = jnp.zeros_like(ref)
    none = jnp.zeros((8, C), BF16)
    for net, w1, w2, pr in ((0, t_w1, t_w2, t_pr), (1, s_w1, s_w2, s_pr)):
        joined[...] = jnp.zeros_like(joined)
        for t in range(9):
            a, b = divmod(t, 3)
            mixed = lax.dot_general(
                lifts[net], taps[2 * net, t], (((1,), (1,)), ((), ())),
                preferred_element_type=F32,
            )
            for side in range(2):
                at = a * 32 + (b + side) * 8
                joined[at : at + 8, side * C : (side + 1) * C] = mixed
            place(w2, t, taps[2 * net + 1, t].T)
        high = joined[...].astype(BF16)
        w1[0:128] = high
        w1[128:256] = (joined[...] - high.astype(F32)).astype(BF16)
        w2[12 * C + 40 : 12 * C + 56] = jnp.concatenate(
            [
                jnp.concatenate([lifts[net], none], axis=1),
                jnp.concatenate([none, lifts[net]], axis=1),
            ],
            axis=0,
        )
        flat_lane = lax.broadcasted_iota(jnp.int32, (128, 128), 1)
        flat_row = lax.broadcasted_iota(jnp.int32, (8, 128), 0)
        flat_col = lax.broadcasted_iota(jnp.int32, (8, 128), 1)
        pick = jnp.where((flat_col % 8 == flat_row) & (flat_row < 4), 1.0, 0.0).astype(BF16)
        wide = lax.dot_general(
            projs[net], pick, (((0,), (0,)), ((), ())), preferred_element_type=F32
        )
        slot = flat_lane % 32 // 8
        odd_slot = (slot == 0) | (slot == 2)
        inside = flat_lane < 96
        pr[0:C] = jnp.where(inside & jnp.logical_not(odd_slot), wide, 0.0).astype(BF16)
        pr[C : 2 * C] = jnp.where(inside & odd_slot, wide, 0.0).astype(BF16)
    for t in range(9):
        place(s_r, t, taps[3, 8 - t])
    s_pt[...] = jnp.zeros_like(s_pt)
    s_pt[40:56] = jnp.concatenate(
        [
            jnp.concatenate([projs[1], none], axis=1),
            jnp.concatenate([none, projs[1]], axis=1),
        ],
        axis=0,
    )

    def spread(value, ref, r, nb):
        for n in range(nb):
            row = value[n]
            ref[r + n, :, 0:128] = pltpu.roll(row[:, 128:], 1, 0).astype(BF16)
            ref[r + n, :, 128:384] = row.astype(BF16)
            ref[r + n, :, 384:512] = pltpu.roll(row[:, :128], pairs - 1, 0).astype(BF16)

    def conv1(state, q_inv, w1, first, last, nb, save):
        scale = jnp.where(is_x, q_inv, 1.0)

        def body(r):
            xs = state[pl.ds(r - 1, nb + 2)] * scale
            shifted = []
            for n in range(nb + 2):
                row = xs[n]
                back = pltpu.roll(row, 1, 0)
                ahead = pltpu.roll(row, pairs - 1, 0)
                shifted.append(jnp.where(lane_j[0] == 0, back, jnp.where(lane_j[0] == 3, ahead, row)))
            u = jnp.stack(
                [
                    jnp.where(
                        lane_a[0] == 0,
                        shifted[n],
                        jnp.where(lane_a[0] == 1, shifted[n + 1], shifted[n + 2]),
                    )
                    for n in range(nb)
                ]
            ).astype(BF16)
            u2[pl.ds(r, nb)] = u
            flat = u.reshape(nb * pairs, 128)
            pre = jnp.dot(
                jnp.concatenate([flat, flat], axis=1), w1[...], preferred_element_type=F32
            ).reshape(nb, pairs, 256)
            spread(silu(pre), x4, r, nb)
            if save:
                slope1[pl.ds(r, nb)] = silu_slope(pre)

        blocks(first, last, nb, body)
        zero_edges(x4)

    def conv2(w2, pr, first, last, nb, save):
        def body(r):
            lhs = jnp.concatenate(
                [x4[pl.ds(r + a - 1, nb)].reshape(nb * pairs, 512) for a in range(3)]
                + [u2[pl.ds(r, nb)].reshape(nb * pairs, 128)],
                axis=1,
            )
            z = jnp.dot(lhs, w2[...], preferred_element_type=F32)
            g = silu(z).astype(BF16)
            fld[pl.ds(r, nb)] = jnp.dot(g, pr[...], preferred_element_type=F32).reshape(
                nb, pairs, 128
            )
            if save:
                slope2[pl.ds(r, nb)] = silu_slope(z).reshape(nb, pairs, 256)

        blocks(first, last, nb, body)
        zero_edges(fld)

    s0, s1, s2 = sc[0], sc[1], sc[2]
    q_inv = [sc[3], sc[4], sc[5]]
    rest = [sc[6], sc[7], sc[8]]
    keep = [sc[9], sc[10], sc[11]]
    gain = [sc[12], sc[13], sc[14]]
    h0, h1 = sc[15], sc[16]
    h0_a, h0_b, h1_b, h1_c = sc[17], sc[18], sc[19], sc[20]
    back = sc[21]
    pull = sc[22]

    def teacher(state, level, first):
        last = total - first
        conv1(state, q_inv[level], t_w1, first, last, 4, False)
        conv2(t_w2, t_pr, first + 1, last - 1, 6, False)

    def update(dst, first, fn):
        def body(r):
            at = pl.ds(r, 2)
            dst[at] = fn(at)

        blocks(first, total - first, 2, body)

    def euler(src, dst, first, level, ratio):
        cx = jnp.where(is_x, 1.0 + ratio * rest[level], 1.0)
        cf = ratio * gain[level]
        update(dst, first, lambda at: src[at] * cx - fld[at] * cf)

    def correct(src, guess, dst, first, level, ratio):
        cx = jnp.where(is_x, 0.5 + 0.5 * ratio * rest[level], 0.5)
        cf = 0.5 * ratio * gain[level]
        update(dst, first, lambda at: 0.5 * src[at] + guess[at] * cx - fld[at] * cf)

    teacher(x0, 0, 1)
    euler(x0, xa, 2, 0, h0_a)
    teacher(xa, 1, 3)
    correct(x0, xa, xb, 4, 1, h0_b)
    teacher(xb, 1, 5)
    euler(xb, xa, 6, 1, h1_b)
    teacher(xa, 2, 7)
    correct(xb, xa, xb, 8, 2, h1_c)

    def make_target(at):
        start = x0[at]
        return start - (xb[at] - start) * back

    update(xa, 8, make_target)

    def emit(i, carry):
        row = xa[HALO + i]
        turned[pl.ds(0, pairs, stride=2)] = row
        turned[pl.ds(1, pairs, stride=2)] = pltpu.roll(row, 120, 1)
        flat = turned[0:cols].T
        tgt_ref[:, i, :] = flat[8:12]
        return carry

    lax.fori_loop(0, rows, emit, 0)

    conv1(x0, q_inv[0], s_w1, 7, total - 7, 4, True)
    conv2(s_w2, s_pr, 8, total - 8, 6, True)

    def backward(r):
        at = pl.ds(r, 2)
        d_field = jnp.where(
            is_x, pull * (keep[0] * x0[at] + gain[0] * fld[at] - xa[at]), 0.0
        ).astype(BF16)
        d_gated = jnp.dot(
            d_field.reshape(2 * pairs, 128), s_pt[...], preferred_element_type=F32
        ).reshape(2, pairs, 256)
        spread(d_gated * slope2[at], dz4, r, 2)

    blocks(8, total - 8, 2, backward)
    zero_edges(dz4)

    cells = rows * center
    dims = (((0,), (0,)), ((), ()))
    middle = pl.ds(HALO, rows)
    dz = dz4[middle, 0:center, 128:384].reshape(cells, 256)
    for a in range(3):
        near = x4[pl.ds(HALO - 1 + a, rows), 0:center, :].reshape(cells, 512)
        grad = lax.dot_general(dz, near, dims, preferred_element_type=F32)
        for b in range(3):
            sum_ref[3 * a + b] = (
                grad[:128, b * C : (b + 1) * C] + grad[128:, (b + 1) * C : (b + 2) * C]
            )

    def conv3(r):
        lhs = jnp.concatenate(
            [dz4[pl.ds(r + a - 1, 4)].reshape(4 * pairs, 512) for a in range(3)], axis=1
        )
        dh = jnp.dot(lhs, s_r[...], preferred_element_type=F32).reshape(4, pairs, 256)
        dpre[pl.ds(r - HALO, 4)] = (dh * slope1[pl.ds(r, 4)]).astype(BF16)

    blocks(HALO, HALO + rows, 4, conv3)
    d_before = dpre[:, 0:center, :].reshape(cells, 256)
    near = u2[middle, 0:center, :].reshape(cells, 128)
    grad = lax.dot_general(d_before, near, dims, preferred_element_type=F32)
    sum_ref[9] = grad[:128] + pltpu.roll(grad[128:], 120, 1)


def local(
    clean, noise, mean_field, sigma_index,
    teacher_lift, teacher_first, teacher_second, teacher_proj,
    student_lift, student_first, student_second, student_proj,
):
    rows, cols = clean.shape[1:]
    lat_n, lon_n = lax.axis_size("lat"), lax.axis_size("lon")
    total, pairs, center = rows + 2 * HALO, (cols + 2 * SIDE) // 2, cols // 2
    vmem = pl.BlockSpec(memory_space=pltpu.VMEM)
    smem = pl.BlockSpec(memory_space=pltpu.SMEM)
    table = jnp.asarray(scalar_table().reshape(-1))

    offsets = [0, 1] if lon_n == 2 else [0, 1, -1]
    slots = len(offsets)
    links = 3 * slots - 1
    blocks = pl.pallas_call(
        functools.partial(halo_kernel, lat_n, lon_n, offsets),
        out_shape=jax.ShapeDtypeStruct((3, slots, 8, rows, cols), F32),
        in_specs=[smem, smem, vmem, vmem, vmem],
        out_specs=vmem,
        scratch_shapes=[pltpu.SemaphoreType.DMA((links,)), pltpu.SemaphoreType.DMA((links,))],
        compiler_params=pltpu.CompilerParams(
            collective_id=0, has_side_effects=True, vmem_limit_bytes=16 * 1024 * 1024
        ),
    )(table, sigma_index, clean, noise, mean_field)

    taps = jnp.stack(
        [teacher_first, teacher_second, student_first, student_second]
    ).transpose(0, 2, 1, 3)
    lifts = jnp.stack([teacher_lift, student_lift]).transpose(0, 2, 1)
    projs = jnp.pad(jnp.stack([teacher_proj, student_proj]), ((0, 0), (0, 4), (0, 0)))
    target, sums = pl.pallas_call(
        functools.partial(kernel, rows, pairs, center),
        out_shape=[
            jax.ShapeDtypeStruct((4, rows, cols), F32),
            jax.ShapeDtypeStruct((10, C, C), F32),
        ],
        in_specs=[smem, smem] + [vmem] * 4,
        out_specs=[vmem] * 2,
        scratch_shapes=[pltpu.VMEM((total, pairs, 128), F32)] * 4
        + [
            pltpu.VMEM((total, pairs, 128), BF16),
            pltpu.VMEM((total, pairs, 512), BF16),
            pltpu.VMEM((total, pairs, 512), BF16),
            pltpu.VMEM((total, pairs, 256), F32),
            pltpu.VMEM((total, pairs, 256), F32),
            pltpu.VMEM((rows, pairs, 256), BF16),
        ]
        + [
            pltpu.VMEM((2 * C, 2 * C), BF16),
            pltpu.VMEM((13 * C, 2 * C), BF16),
            pltpu.VMEM((2 * C, C), BF16),
        ]
        * 2
        + [
            pltpu.VMEM((12 * C, 2 * C), BF16),
            pltpu.VMEM((C, 2 * C), BF16),
            pltpu.VMEM((C, 2 * C), F32),
            pltpu.VMEM((2 * pairs, 128), F32),
        ],
        compiler_params=pltpu.CompilerParams(vmem_limit_bytes=56 * 1024 * 1024),
    )(table, sigma_index, blocks, taps, lifts, projs)

    inner = 4 if lat_n % 4 == 0 else 1
    depth, plane = lat_n // inner, inner * lon_n
    piece = -(-10 * C // (plane * depth * 8)) * 8
    while piece * depth % 16:
        piece += 8
    chunk = piece * depth
    part = sums.reshape(10 * C, C)
    if plane * chunk > 10 * C:
        part = jnp.pad(part, ((0, plane * chunk - 10 * C), (0, 0)))
    links = 2 * (plane + depth - 2)
    update_first, update_second = pl.pallas_call(
        functools.partial(sum_kernel, inner, depth, lon_n, chunk, piece),
        out_shape=[jax.ShapeDtypeStruct((C, 9, C), F32)] * 2,
        in_specs=[vmem] * 2,
        out_specs=[vmem] * 2,
        scratch_shapes=[
            pltpu.VMEM((plane, chunk, 128), BF16),
            pltpu.VMEM((plane - 1, chunk, 128), BF16),
            pltpu.VMEM((depth, piece, 128), F32),
            pltpu.VMEM((depth - 1, piece, 128), F32),
            pltpu.VMEM((depth, piece, 128), F32),
            pltpu.VMEM((plane, chunk, 128), BF16),
            pltpu.SemaphoreType.DMA((links,)),
            pltpu.SemaphoreType.DMA((links,)),
        ],
        compiler_params=pltpu.CompilerParams(
            collective_id=1, has_side_effects=True, vmem_limit_bytes=32 * 1024 * 1024
        ),
    )(part, student_lift.T.astype(F32))
    return (target, update_first, update_second)


def solution(mesh):
    grid = P(None, "lat", "lon")
    return jax.shard_map(
        local,
        mesh=mesh,
        in_specs=(grid, grid, grid) + (P(),) * 9,
        out_specs=(grid, P(), P()),
        check_vma=False,
    )
```

```python
import functools

import jax
import jax.numpy as jnp
import numpy as np
from jax import lax
from jax.experimental import pallas as pl
from jax.experimental.pallas import tpu as pltpu
from jax.sharding import PartitionSpec as P

SCHED = 18
HALO = 9
SIDE = 16
C = 128
F32 = jnp.float32
BF16 = jnp.bfloat16


def scalar_table():
    ramp = np.arange(SCHED, dtype=np.float64) / (SCHED - 1)
    top, bottom = 80.0 ** (1.0 / 7.0), 0.02 ** (1.0 / 7.0)
    sigma = (top + ramp * (bottom - top)) ** 7.0
    rows = []
    for n in range(SCHED - 2):
        sig = sigma[n : n + 3]
        s0, s1, s2 = sig
        q2 = sig * sig + 0.25
        q = np.sqrt(q2)
        lam = q2[0] / (s0 * s0 * 0.25)
        h0, h1 = s1 - s0, s2 - s1
        rows.append(
            [*sig, *(1.0 / q), *(sig * sig / q2), *(0.25 / q2), *(sig * 0.5 / q)]
            + [h0, h1, h0 / s0, h0 / s1, h1 / s1, h1 / s2, s0 / (s2 - s0)]
            + [s0 * 0.5 / q[0] * 2.0 * lam]
        )
    return np.asarray(rows, np.float32)


N_SCALARS = 23
MESH = pl.DeviceIdType.MESH


def halo_kernel(lat_n, lon_n, offsets, table, index, clean, noise, mean, out, send, recv):
    y, x = lax.axis_index("lat"), lax.axis_index("lon")
    partners = []
    for dy in (0, 1, -1):
        for n, dx in enumerate(offsets):
            if dy or dx:
                back = [(-dx - other) % lon_n for other in offsets].index(0)
                partners.append(
                    (lax.rem(y + dy + lat_n, lat_n), lax.rem(x + dx + lon_n, lon_n), 1 - dy, back)
                )
    barrier = pltpu.get_barrier_semaphore()
    for py, px, _, _ in partners:
        pl.semaphore_signal(barrier, inc=1, device_id=(py, px), device_id_type=MESH)
    out[1, 0, 0:4] = clean[...] + table[index[0] * N_SCALARS] * noise[...]
    out[1, 0, 4:8] = mean[...]
    pl.semaphore_wait(barrier, len(partners))
    copies = []
    for k, (py, px, sy, sx) in enumerate(partners):
        copy = pltpu.make_async_remote_copy(
            src_ref=out.at[1, 0],
            dst_ref=out.at[sy, sx],
            send_sem=send.at[k],
            recv_sem=recv.at[k],
            device_id=(py, px),
            device_id_type=MESH,
        )
        copy.start()
        copies.append(copy)
    for copy in copies:
        copy.wait()


def sum_kernel(
    inner, depth, lon_n, chunk, piece,
    part, lift, first_ref, second_ref,
    outgoing, plane_in, held, line_in, line_all, plane_all, send, recv,
):
    y, x = lax.axis_index("lat"), lax.axis_index("lon")
    plane = inner * lon_n
    line = lax.div(y, inner)
    spot = lax.rem(y, inner) * lon_n + x

    def in_plane(step):
        other = lax.rem(spot + step, plane)
        return other, (line * inner + lax.div(other, lon_n), lax.rem(other, lon_n))

    def in_line(step):
        other = lax.rem(line + step, depth)
        return other, (other * inner + lax.rem(y, inner), x)

    barrier = pltpu.get_barrier_semaphore()
    for step in range(1, plane):
        pl.semaphore_signal(barrier, inc=1, device_id=in_plane(step)[1], device_id_type=MESH)
    for step in range(1, depth):
        pl.semaphore_signal(barrier, inc=1, device_id=in_line(step)[1], device_id_type=MESH)
    for n in range(plane):
        outgoing[n] = part[n * chunk : (n + 1) * chunk].astype(BF16)
    pl.semaphore_wait(barrier, plane + depth - 2)

    used = [0]

    def exchange(count, where, source, target):
        copies = []
        for step in range(1, count):
            other, device = where(step)
            k = used[0]
            used[0] += 1
            copy = pltpu.make_async_remote_copy(
                src_ref=source(other),
                dst_ref=target(step),
                send_sem=send.at[k],
                recv_sem=recv.at[k],
                device_id=device,
                device_id_type=MESH,
            )
            copy.start()
            copies.append(copy)
        for copy in copies:
            copy.wait()

    exchange(plane, in_plane, lambda o: outgoing.at[o], lambda step: plane_in.at[step - 1])
    own = part[pl.ds(pl.multiple_of(spot * chunk, 8), chunk)]
    for n in range(plane - 1):
        own = own + plane_in[n].astype(F32)
    for n in range(depth):
        held[n] = own[n * piece : (n + 1) * piece]
    exchange(depth, in_line, lambda o: held.at[o], lambda step: line_in.at[step - 1])
    whole = held[line]
    for n in range(depth - 1):
        whole = whole + line_in[n]
    line_all[line] = whole
    exchange(depth, in_line, lambda o: line_all.at[line], lambda step: line_all.at[line])
    plane_all[spot] = line_all[...].reshape(chunk, 128).astype(BF16)
    exchange(plane, in_plane, lambda o: plane_all.at[spot], lambda step: plane_all.at[spot])

    total = plane_all[...].reshape(plane * chunk, 128).astype(F32)
    size = 1.0 / (9 * C * C)
    second = [total[t * C : (t + 1) * C] for t in range(9)]
    spots = total[9 * C : 10 * C]
    tall = jnp.concatenate([lift[...].astype(F32).T] * 16, axis=0)
    group = lax.broadcasted_iota(jnp.int32, (128, 128), 0) // 8
    first = [
        jnp.dot(
            spots,
            jnp.where(group == 4 * (t // 3) + t % 3, tall, 0.0),
            precision=lax.Precision.HIGHEST,
            preferred_element_type=F32,
        )
        for t in range(9)
    ]
    for blocks, ref in ((first, first_ref), (second, second_ref)):
        squares = blocks[0] * blocks[0]
        for t in range(1, 9):
            squares = squares + blocks[t] * blocks[t]
        factor = lax.rsqrt(jnp.sum(squares, keepdims=True) * size + 1e-06)
        for t in range(9):
            ref[:, t, :] = blocks[t] * factor


def silu(v):
    u = 0.5 * v
    return u + u * jnp.tanh(u)


def silu_slope(v):
    sig = 0.5 + 0.5 * jnp.tanh(0.5 * v)
    return sig * (1.0 + v * (1.0 - sig))


def kernel(
    rows, pairs, center,
    table, index, blocks_in, taps, t_lift, s_lift, t_proj, s_proj,
    tgt_ref, sum_ref,
    x0, xa, xb, fld, u2, x4, dz4, slope1, slope2, dpre,
    t_w1, t_w2, t_pr, s_w1, s_w2, s_pr, s_r, s_pt, joined, turned,
):
    total = rows + 2 * HALO
    me = lax.axis_index("lat")
    top = me == 0
    bottom = me == lax.axis_size("lat") - 1
    base = index[0] * N_SCALARS
    sc = [table[base + k] for k in range(N_SCALARS)]
    lane = lax.broadcasted_iota(jnp.int32, (1, 1, 128), 2)
    lane_a = lane // 32
    lane_j = lane % 32 // 8
    is_x = lane % 8 < 4

    def zero_edges(ref):
        @pl.when(top)
        def _():
            ref[0:HALO] = jnp.zeros((HALO,) + ref.shape[1:], ref.dtype)

        @pl.when(bottom)
        def _():
            ref[HALO + rows : total] = jnp.zeros((HALO,) + ref.shape[1:], ref.dtype)

    def blocks(first, last, size, body):
        count = -(-(last - first) // size)
        room, gaps = last - first - size, max(count - 1, 1)

        def step(i, carry):
            body(first + i * room // gaps)
            return carry

        lax.fori_loop(0, count, step, 0)

    cols = 2 * center
    odd_lane = (lane_j[0] == 0) | (lane_j[0] == 2)
    last_slot = blocks_in.shape[1] - 1
    column = lax.broadcasted_iota(jnp.int32, (8, cols), 1)

    def load_rows(slot, source, first, count):
        def step(i, carry):
            own = blocks_in[slot, 0, :, source + i, :]
            beside = jnp.where(
                column < SIDE,
                blocks_in[slot, 1, :, source + i, :],
                blocks_in[slot, last_slot, :, source + i, :],
            )
            turned[0:cols] = jnp.concatenate([own] * 16, axis=0).T
            sides = jnp.concatenate([beside] * 16, axis=0).T
            turned[cols : cols + SIDE] = sides[:SIDE]
            turned[cols + SIDE : cols + 2 * SIDE] = sides[cols - SIDE :]
            even = turned[pl.ds(0, pairs, stride=2)]
            odd = turned[pl.ds(1, pairs, stride=2)]
            x0[first + i] = jnp.where(odd_lane, odd, even)
            return carry

        lax.fori_loop(0, count, step, 0)

    load_rows(0, rows - HALO, 0, HALO)
    load_rows(1, 0, HALO, rows)
    load_rows(2, 0, HALO + rows, HALO)
    zero_edges(x0)

    def place(ref, t, block):
        a, b = divmod(t, 3)
        for side in range(2):
            at = (4 * a + b + side) * C
            ref[at : at + C, side * C : (side + 1) * C] = block

    for ref in (t_w2, s_w2, s_r):
        ref[...] = jnp.zeros_like(ref)
    none = jnp.zeros((8, C), BF16)
    four = jnp.zeros((4, C), F32)
    lifts = [ref[...].astype(F32).T.astype(BF16) for ref in (t_lift, s_lift)]
    projs = [
        jnp.concatenate([ref[...].astype(F32), four], axis=0).astype(BF16)
        for ref in (t_proj, s_proj)
    ]
    for net, w1, w2, pr in ((0, t_w1, t_w2, t_pr), (1, s_w1, s_w2, s_pr)):
        joined[...] = jnp.zeros_like(joined)
        for t in range(9):
            a, b = divmod(t, 3)
            mixed = lax.dot_general(
                lifts[net], taps[2 * net, t], (((1,), (1,)), ((), ())),
                preferred_element_type=F32,
            )
            for side in range(2):
                at = a * 32 + (b + side) * 8
                joined[at : at + 8, side * C : (side + 1) * C] = mixed
            place(w2, t, taps[2 * net + 1, t].T)
        high = joined[...].astype(BF16)
        w1[0:128] = high
        w1[128:256] = (joined[...] - high.astype(F32)).astype(BF16)
        w2[12 * C + 40 : 12 * C + 56] = jnp.concatenate(
            [
                jnp.concatenate([lifts[net], none], axis=1),
                jnp.concatenate([none, lifts[net]], axis=1),
            ],
            axis=0,
        )
        flat_lane = lax.broadcasted_iota(jnp.int32, (128, 128), 1)
        flat_row = lax.broadcasted_iota(jnp.int32, (8, 128), 0)
        flat_col = lax.broadcasted_iota(jnp.int32, (8, 128), 1)
        pick = jnp.where((flat_col % 8 == flat_row) & (flat_row < 4), 1.0, 0.0).astype(BF16)
        wide = lax.dot_general(
            projs[net], pick, (((0,), (0,)), ((), ())), preferred_element_type=F32
        )
        slot = flat_lane % 32 // 8
        odd_slot = (slot == 0) | (slot == 2)
        inside = flat_lane < 96
        pr[0:C] = jnp.where(inside & jnp.logical_not(odd_slot), wide, 0.0).astype(BF16)
        pr[C : 2 * C] = jnp.where(inside & odd_slot, wide, 0.0).astype(BF16)
    for t in range(9):
        place(s_r, t, taps[3, 8 - t])
    s_pt[...] = jnp.zeros_like(s_pt)
    s_pt[40:56] = jnp.concatenate(
        [
            jnp.concatenate([projs[1], none], axis=1),
            jnp.concatenate([none, projs[1]], axis=1),
        ],
        axis=0,
    )

    def spread(value, ref, r, nb):
        for n in range(nb):
            row = value[n]
            ref[r + n, :, 0:128] = pltpu.roll(row[:, 128:], 1, 0).astype(BF16)
            ref[r + n, :, 128:384] = row.astype(BF16)
            ref[r + n, :, 384:512] = pltpu.roll(row[:, :128], pairs - 1, 0).astype(BF16)

    def conv1(state, q_inv, w1, first, last, nb, save):
        scale = jnp.where(is_x, q_inv, 1.0)

        def body(r):
            xs = state[pl.ds(r - 1, nb + 2)] * scale
            shifted = []
            for n in range(nb + 2):
                row = xs[n]
                back = pltpu.roll(row, 1, 0)
                ahead = pltpu.roll(row, pairs - 1, 0)
                shifted.append(jnp.where(lane_j[0] == 0, back, jnp.where(lane_j[0] == 3, ahead, row)))
            u = jnp.stack(
                [
                    jnp.where(
                        lane_a[0] == 0,
                        shifted[n],
                        jnp.where(lane_a[0] == 1, shifted[n + 1], shifted[n + 2]),
                    )
                    for n in range(nb)
                ]
            ).astype(BF16)
            u2[pl.ds(r, nb)] = u
            flat = u.reshape(nb * pairs, 128)
            pre = jnp.dot(
                jnp.concatenate([flat, flat], axis=1), w1[...], preferred_element_type=F32
            ).reshape(nb, pairs, 256)
            spread(silu(pre), x4, r, nb)
            if save:
                slope1[pl.ds(r, nb)] = silu_slope(pre)

        blocks(first, last, nb, body)
        zero_edges(x4)

    def conv2(w2, pr, first, last, nb, save):
        def body(r):
            lhs = jnp.concatenate(
                [x4[pl.ds(r + a - 1, nb)].reshape(nb * pairs, 512) for a in range(3)]
                + [u2[pl.ds(r, nb)].reshape(nb * pairs, 128)],
                axis=1,
            )
            z = jnp.dot(lhs, w2[...], preferred_element_type=F32)
            g = silu(z).astype(BF16)
            fld[pl.ds(r, nb)] = jnp.dot(g, pr[...], preferred_element_type=F32).reshape(
                nb, pairs, 128
            )
            if save:
                slope2[pl.ds(r, nb)] = silu_slope(z).reshape(nb, pairs, 256)

        blocks(first, last, nb, body)
        zero_edges(fld)

    s0, s1, s2 = sc[0], sc[1], sc[2]
    q_inv = [sc[3], sc[4], sc[5]]
    rest = [sc[6], sc[7], sc[8]]
    keep = [sc[9], sc[10], sc[11]]
    gain = [sc[12], sc[13], sc[14]]
    h0, h1 = sc[15], sc[16]
    h0_a, h0_b, h1_b, h1_c = sc[17], sc[18], sc[19], sc[20]
    back = sc[21]
    pull = sc[22]

    def teacher(state, level, first):
        last = total - first
        conv1(state, q_inv[level], t_w1, first, last, 8, False)
        conv2(t_w2, t_pr, first + 1, last - 1, 6, False)

    def update(dst, first, fn):
        def body(r):
            at = pl.ds(r, 2)
            dst[at] = fn(at)

        blocks(first, total - first, 2, body)

    def euler(src, dst, first, level, ratio):
        cx = jnp.where(is_x, 1.0 + ratio * rest[level], 1.0)
        cf = ratio * gain[level]
        update(dst, first, lambda at: src[at] * cx - fld[at] * cf)

    def correct(src, guess, dst, first, level, ratio):
        cx = jnp.where(is_x, 0.5 + 0.5 * ratio * rest[level], 0.5)
        cf = 0.5 * ratio * gain[level]
        update(dst, first, lambda at: 0.5 * src[at] + guess[at] * cx - fld[at] * cf)

    teacher(x0, 0, 1)
    euler(x0, xa, 2, 0, h0_a)
    teacher(xa, 1, 3)
    correct(x0, xa, xb, 4, 1, h0_b)
    teacher(xb, 1, 5)
    euler(xb, xa, 6, 1, h1_b)
    teacher(xa, 2, 7)
    correct(xb, xa, xb, 8, 2, h1_c)

    def make_target(at):
        start = x0[at]
        return start - (xb[at] - start) * back

    update(xa, 8, make_target)

    for first in range(0, rows, 16):
        count = min(16, rows - first)
        even = jnp.zeros((center, 128), F32)
        odd = even
        group = lax.broadcasted_iota(jnp.int32, (center, 128), 1) // 8
        for i in range(count):
            row = xa[HALO + first + i, 0:center]
            even = jnp.where(group == i, pltpu.roll(row, (8 * i + 120) % 128, 1), even)
            odd = jnp.where(group == i, pltpu.roll(row, (8 * i + 112) % 128, 1), odd)
        turned[pl.ds(0, center, stride=2)] = even
        turned[pl.ds(1, center, stride=2)] = odd
        flat = turned[0:cols].T
        for i in range(count):
            tgt_ref[:, first + i, :] = flat[8 * i : 8 * i + 4]

    conv1(x0, q_inv[0], s_w1, 7, total - 7, 4, True)
    conv2(s_w2, s_pr, 8, total - 8, 6, True)

    def backward(r):
        at = pl.ds(r, 2)
        d_field = jnp.where(
            is_x, pull * (keep[0] * x0[at] + gain[0] * fld[at] - xa[at]), 0.0
        ).astype(BF16)
        d_gated = jnp.dot(
            d_field.reshape(2 * pairs, 128), s_pt[...], preferred_element_type=F32
        ).reshape(2, pairs, 256)
        spread(d_gated * slope2[at], dz4, r, 2)

    blocks(8, total - 8, 2, backward)
    zero_edges(dz4)

    cells = rows * center
    dims = (((0,), (0,)), ((), ()))
    middle = pl.ds(HALO, rows)
    dz = dz4[middle, 0:center, 128:384].reshape(cells, 256)
    for a in range(3):
        near = x4[pl.ds(HALO - 1 + a, rows), 0:center, :].reshape(cells, 512)
        grad = lax.dot_general(dz, near, dims, preferred_element_type=F32)
        for b in range(3):
            sum_ref[3 * a + b] = (
                grad[:128, b * C : (b + 1) * C] + grad[128:, (b + 1) * C : (b + 2) * C]
            )

    def conv3(r):
        lhs = jnp.concatenate(
            [dz4[pl.ds(r + a - 1, 4)].reshape(4 * pairs, 512) for a in range(3)], axis=1
        )
        dh = jnp.dot(lhs, s_r[...], preferred_element_type=F32).reshape(4, pairs, 256)
        dpre[pl.ds(r - HALO, 4)] = (dh * slope1[pl.ds(r, 4)]).astype(BF16)

    blocks(HALO, HALO + rows, 4, conv3)
    d_before = dpre[:, 0:center, :].reshape(cells, 256)
    near = u2[middle, 0:center, :].reshape(cells, 128)
    grad = lax.dot_general(d_before, near, dims, preferred_element_type=F32)
    sum_ref[9] = grad[:128] + pltpu.roll(grad[128:], 120, 1)


def local(
    clean, noise, mean_field, sigma_index,
    teacher_lift, teacher_first, teacher_second, teacher_proj,
    student_lift, student_first, student_second, student_proj,
):
    rows, cols = clean.shape[1:]
    lat_n, lon_n = lax.axis_size("lat"), lax.axis_size("lon")
    total, pairs, center = rows + 2 * HALO, (cols + 2 * SIDE) // 2, cols // 2
    vmem = pl.BlockSpec(memory_space=pltpu.VMEM)
    smem = pl.BlockSpec(memory_space=pltpu.SMEM)
    table = jnp.asarray(scalar_table().reshape(-1))

    offsets = [0, 1] if lon_n == 2 else [0, 1, -1]
    slots = len(offsets)
    links = 3 * slots - 1
    blocks = pl.pallas_call(
        functools.partial(halo_kernel, lat_n, lon_n, offsets),
        out_shape=jax.ShapeDtypeStruct((3, slots, 8, rows, cols), F32),
        in_specs=[smem, smem, vmem, vmem, vmem],
        out_specs=vmem,
        scratch_shapes=[pltpu.SemaphoreType.DMA((links,)), pltpu.SemaphoreType.DMA((links,))],
        compiler_params=pltpu.CompilerParams(
            collective_id=0, has_side_effects=True, vmem_limit_bytes=16 * 1024 * 1024
        ),
    )(table, sigma_index, clean, noise, mean_field)

    taps = jnp.stack(
        [teacher_first, teacher_second, student_first, student_second]
    ).transpose(0, 2, 1, 3)
    target, sums = pl.pallas_call(
        functools.partial(kernel, rows, pairs, center),
        out_shape=[
            jax.ShapeDtypeStruct((4, rows, cols), F32),
            jax.ShapeDtypeStruct((10, C, C), F32),
        ],
        in_specs=[smem, smem] + [vmem] * 6,
        out_specs=[vmem] * 2,
        scratch_shapes=[pltpu.VMEM((total, pairs, 128), F32)] * 4
        + [
            pltpu.VMEM((total, pairs, 128), BF16),
            pltpu.VMEM((total, pairs, 512), BF16),
            pltpu.VMEM((total, pairs, 512), BF16),
            pltpu.VMEM((total, pairs, 256), F32),
            pltpu.VMEM((total, pairs, 256), F32),
            pltpu.VMEM((rows, pairs, 256), BF16),
        ]
        + [
            pltpu.VMEM((2 * C, 2 * C), BF16),
            pltpu.VMEM((13 * C, 2 * C), BF16),
            pltpu.VMEM((2 * C, C), BF16),
        ]
        * 2
        + [
            pltpu.VMEM((12 * C, 2 * C), BF16),
            pltpu.VMEM((C, 2 * C), BF16),
            pltpu.VMEM((C, 2 * C), F32),
            pltpu.VMEM((2 * pairs, 128), F32),
        ],
        compiler_params=pltpu.CompilerParams(vmem_limit_bytes=56 * 1024 * 1024),
    )(
        table, sigma_index, blocks, taps,
        teacher_lift, student_lift, teacher_proj, student_proj,
    )

    inner = 4 if lat_n % 4 == 0 else 1
    depth, plane = lat_n // inner, inner * lon_n
    piece = -(-10 * C // (plane * depth * 8)) * 8
    while piece * depth % 16:
        piece += 8
    chunk = piece * depth
    part = sums.reshape(10 * C, C)
    if plane * chunk > 10 * C:
        part = jnp.pad(part, ((0, plane * chunk - 10 * C), (0, 0)))
    links = 2 * (plane + depth - 2)
    update_first, update_second = pl.pallas_call(
        functools.partial(sum_kernel, inner, depth, lon_n, chunk, piece),
        out_shape=[jax.ShapeDtypeStruct((C, 9, C), F32)] * 2,
        in_specs=[vmem] * 2,
        out_specs=[vmem] * 2,
        scratch_shapes=[
            pltpu.VMEM((plane, chunk, 128), BF16),
            pltpu.VMEM((plane - 1, chunk, 128), BF16),
            pltpu.VMEM((depth, piece, 128), F32),
            pltpu.VMEM((depth - 1, piece, 128), F32),
            pltpu.VMEM((depth, piece, 128), F32),
            pltpu.VMEM((plane, chunk, 128), BF16),
            pltpu.SemaphoreType.DMA((links,)),
            pltpu.SemaphoreType.DMA((links,)),
        ],
        compiler_params=pltpu.CompilerParams(
            collective_id=1, has_side_effects=True, vmem_limit_bytes=32 * 1024 * 1024
        ),
    )(part, student_lift)
    return (target, update_first, update_second)


def solution(mesh):
    grid = P(None, "lat", "lon")
    return jax.shard_map(
        local,
        mesh=mesh,
        in_specs=(grid, grid, grid) + (P(),) * 9,
        out_specs=(grid, P(), P()),
        check_vma=False,
    )
```

```python
import functools

import jax
import jax.numpy as jnp
import numpy as np
from jax import lax
from jax.experimental import pallas as pl
from jax.experimental.pallas import tpu as pltpu
from jax.sharding import PartitionSpec as P

SCHED = 18
HALO = 9
SIDE = 16
C = 128
F32 = jnp.float32
BF16 = jnp.bfloat16


def scalar_table():
    ramp = np.arange(SCHED, dtype=np.float64) / (SCHED - 1)
    top, bottom = 80.0 ** (1.0 / 7.0), 0.02 ** (1.0 / 7.0)
    sigma = (top + ramp * (bottom - top)) ** 7.0
    rows = []
    for n in range(SCHED - 2):
        sig = sigma[n : n + 3]
        s0, s1, s2 = sig
        q2 = sig * sig + 0.25
        q = np.sqrt(q2)
        lam = q2[0] / (s0 * s0 * 0.25)
        h0, h1 = s1 - s0, s2 - s1
        rows.append(
            [*sig, *(1.0 / q), *(sig * sig / q2), *(0.25 / q2), *(sig * 0.5 / q)]
            + [h0, h1, h0 / s0, h0 / s1, h1 / s1, h1 / s2, s0 / (s2 - s0)]
            + [s0 * 0.5 / q[0] * 2.0 * lam]
        )
    return np.asarray(rows, np.float32)


N_SCALARS = 23
MESH = pl.DeviceIdType.MESH


def silu(v):
    u = 0.5 * v
    return u + u * jnp.tanh(u)


def silu_slope(v):
    sig = 0.5 + 0.5 * jnp.tanh(0.5 * v)
    return sig * (1.0 + v * (1.0 - sig))


def kernel(
    rows, pairs, center, lat_n, lon_n, offsets, inner, chunk_a, chunk_b,
    table, index, clean, noise, mean, t_first, t_second, s_first, s_second,
    t_lift, s_lift, t_proj, s_proj,
    tgt_ref, first_ref, second_ref,
    x0, xa, xb, fld, u2, x4, dz4, slope1, slope2, dpre,
    t_w1, t_w2, t_pr, s_w1, s_w2, s_pr, s_r, s_pt, joined, turned,
    blocks_in, sum_a, sum_b, out_a, out_b, in_a, in_b, held, line_in, line_all, plane_all,
    send, recv,
):
    total = rows + 2 * HALO
    y, x = lax.axis_index("lat"), lax.axis_index("lon")
    top = y == 0
    bottom = y == lat_n - 1
    depth, plane = lat_n // inner, inner * lon_n
    chunk = chunk_a + chunk_b
    piece = chunk // depth
    line = lax.div(y, inner)
    spot = lax.rem(y, inner) * lon_n + x
    beside = []
    for dy in (0, 1, -1):
        for dx in offsets:
            if dy or dx:
                slot = [(-dx - other) % lon_n for other in offsets].index(0)
                device = (lax.rem(y + dy + lat_n, lat_n), lax.rem(x + dx + lon_n, lon_n))
                beside.append((device, 1 - dy, slot))

    def in_plane(step):
        other = lax.rem(spot + step, plane)
        return other, (line * inner + lax.div(other, lon_n), lax.rem(other, lon_n))

    def in_line(step):
        other = lax.rem(line + step, depth)
        return other, (other * inner + lax.rem(y, inner), x)

    greeted = [device for device, _, _ in beside]
    greeted += [in_plane(step)[1] for step in range(1, plane)]
    greeted += [in_line(step)[1] for step in range(1, depth)]
    barrier = pltpu.get_barrier_semaphore()
    for device in greeted:
        pl.semaphore_signal(barrier, inc=1, device_id=device, device_id_type=MESH)
    used = [0]

    def push(source, target, device):
        k = used[0]
        used[0] += 1
        copy = pltpu.make_async_remote_copy(
            src_ref=source, dst_ref=target, send_sem=send.at[k], recv_sem=recv.at[k],
            device_id=device, device_id_type=MESH,
        )
        copy.start()
        return copy

    def exchange(count, where, source, target):
        copies = []
        for step in range(1, count):
            other, device = where(step)
            copies.append(push(source(other), target(step), device))
        return copies

    base = index[0] * N_SCALARS
    sc = [table[base + k] for k in range(N_SCALARS)]
    blocks_in[1, 0, 0:4] = clean[...] + sc[0] * noise[...]
    blocks_in[1, 0, 4:8] = mean[...]
    pl.semaphore_wait(barrier, len(greeted))
    halos = [push(blocks_in.at[1, 0], blocks_in.at[sy, sx], device) for device, sy, sx in beside]
    lane = lax.broadcasted_iota(jnp.int32, (1, 1, 128), 2)
    lane_a = lane // 32
    lane_j = lane % 32 // 8
    is_x = lane % 8 < 4

    def zero_edges(ref):
        @pl.when(top)
        def _():
            ref[0:HALO] = jnp.zeros((HALO,) + ref.shape[1:], ref.dtype)

        @pl.when(bottom)
        def _():
            ref[HALO + rows : total] = jnp.zeros((HALO,) + ref.shape[1:], ref.dtype)

    def blocks(first, last, size, body):
        count = -(-(last - first) // size)
        room, gaps = last - first - size, max(count - 1, 1)

        def step(i, carry):
            body(first + i * room // gaps)
            return carry

        lax.fori_loop(0, count, step, 0)

    def place(ref, t, block):
        a, b = divmod(t, 3)
        for side in range(2):
            at = (4 * a + b + side) * C
            ref[at : at + C, side * C : (side + 1) * C] = block

    for ref in (t_w2, s_w2, s_r):
        ref[...] = jnp.zeros_like(ref)
    none = jnp.zeros((8, C), BF16)
    four = jnp.zeros((4, C), F32)
    lifts = [t_lift[...], s_lift[...]]
    taps = [t_first, t_second, s_first, s_second]
    projs = [
        jnp.concatenate([ref[...].astype(F32), four], axis=0).astype(BF16)
        for ref in (t_proj, s_proj)
    ]
    for net, w1, w2, pr in ((0, t_w1, t_w2, t_pr), (1, s_w1, s_w2, s_pr)):
        joined[...] = jnp.zeros_like(joined)
        for t in range(9):
            a, b = divmod(t, 3)
            mixed = lax.dot_general(
                lifts[net], taps[2 * net][t], (((1,), (1,)), ((), ())),
                preferred_element_type=F32,
            )
            for side in range(2):
                at = a * 32 + (b + side) * 8
                joined[at : at + 8, side * C : (side + 1) * C] = mixed
            place(w2, t, taps[2 * net + 1][t].T)
        high = joined[...].astype(BF16)
        w1[0:128] = high
        w1[128:256] = (joined[...] - high.astype(F32)).astype(BF16)
        w2[12 * C + 40 : 12 * C + 56] = jnp.concatenate(
            [
                jnp.concatenate([lifts[net], none], axis=1),
                jnp.concatenate([none, lifts[net]], axis=1),
            ],
            axis=0,
        )
        flat_lane = lax.broadcasted_iota(jnp.int32, (128, 128), 1)
        flat_row = lax.broadcasted_iota(jnp.int32, (8, 128), 0)
        flat_col = lax.broadcasted_iota(jnp.int32, (8, 128), 1)
        pick = jnp.where((flat_col % 8 == flat_row) & (flat_row < 4), 1.0, 0.0).astype(BF16)
        wide = lax.dot_general(
            projs[net], pick, (((0,), (0,)), ((), ())), preferred_element_type=F32
        )
        slot = flat_lane % 32 // 8
        odd_slot = (slot == 0) | (slot == 2)
        inside = flat_lane < 96
        pr[0:C] = jnp.where(inside & jnp.logical_not(odd_slot), wide, 0.0).astype(BF16)
        pr[C : 2 * C] = jnp.where(inside & odd_slot, wide, 0.0).astype(BF16)
    for t in range(9):
        place(s_r, t, taps[3][8 - t])
    s_pt[...] = jnp.zeros_like(s_pt)
    s_pt[40:56] = jnp.concatenate(
        [
            jnp.concatenate([projs[1], none], axis=1),
            jnp.concatenate([none, projs[1]], axis=1),
        ],
        axis=0,
    )

    for copy in halos:
        copy.wait()

    cols = 2 * center
    odd_lane = (lane_j[0] == 0) | (lane_j[0] == 2)
    last_slot = blocks_in.shape[1] - 1
    column = lax.broadcasted_iota(jnp.int32, (8, cols), 1)

    def load_rows(slot, source, first, count):
        def step(i, carry):
            own = blocks_in[slot, 0, :, source + i, :]
            sides = jnp.where(
                column < SIDE,
                blocks_in[slot, 1, :, source + i, :],
                blocks_in[slot, last_slot, :, source + i, :],
            )
            turned[0:cols] = jnp.concatenate([own] * 16, axis=0).T
            sides = jnp.concatenate([sides] * 16, axis=0).T
            turned[cols : cols + SIDE] = sides[:SIDE]
            turned[cols + SIDE : cols + 2 * SIDE] = sides[cols - SIDE :]
            even = turned[pl.ds(0, pairs, stride=2)]
            odd = turned[pl.ds(1, pairs, stride=2)]
            x0[first + i] = jnp.where(odd_lane, odd, even)
            return carry

        lax.fori_loop(0, count, step, 0)

    load_rows(0, rows - HALO, 0, HALO)
    load_rows(1, 0, HALO, rows)
    load_rows(2, 0, HALO + rows, HALO)
    zero_edges(x0)

    def spread(value, ref, r, nb):
        for n in range(nb):
            row = value[n]
            ref[r + n, :, 0:128] = pltpu.roll(row[:, 128:], 1, 0).astype(BF16)
            ref[r + n, :, 128:384] = row.astype(BF16)
            ref[r + n, :, 384:512] = pltpu.roll(row[:, :128], pairs - 1, 0).astype(BF16)

    def conv1(state, q_inv, w1, first, last, nb, save):
        scale = jnp.where(is_x, q_inv, 1.0)

        def body(r):
            xs = state[pl.ds(r - 1, nb + 2)] * scale
            shifted = []
            for n in range(nb + 2):
                row = xs[n]
                back = pltpu.roll(row, 1, 0)
                ahead = pltpu.roll(row, pairs - 1, 0)
                shifted.append(jnp.where(lane_j[0] == 0, back, jnp.where(lane_j[0] == 3, ahead, row)))
            u = jnp.stack(
                [
                    jnp.where(
                        lane_a[0] == 0,
                        shifted[n],
                        jnp.where(lane_a[0] == 1, shifted[n + 1], shifted[n + 2]),
                    )
                    for n in range(nb)
                ]
            ).astype(BF16)
            u2[pl.ds(r, nb)] = u
            flat = u.reshape(nb * pairs, 128)
            pre = jnp.dot(
                jnp.concatenate([flat, flat], axis=1), w1[...], preferred_element_type=F32
            ).reshape(nb, pairs, 256)
            spread(silu(pre), x4, r, nb)
            if save:
                slope1[pl.ds(r, nb)] = silu_slope(pre)

        blocks(first, last, nb, body)
        zero_edges(x4)

    def conv2(w2, pr, first, last, nb, save):
        def body(r):
            lhs = jnp.concatenate(
                [x4[pl.ds(r + a - 1, nb)].reshape(nb * pairs, 512) for a in range(3)]
                + [u2[pl.ds(r, nb)].reshape(nb * pairs, 128)],
                axis=1,
            )
            z = jnp.dot(lhs, w2[...], preferred_element_type=F32)
            g = silu(z).astype(BF16)
            fld[pl.ds(r, nb)] = jnp.dot(g, pr[...], preferred_element_type=F32).reshape(
                nb, pairs, 128
            )
            if save:
                slope2[pl.ds(r, nb)] = silu_slope(z).reshape(nb, pairs, 256)

        blocks(first, last, nb, body)
        zero_edges(fld)

    s0, s1, s2 = sc[0], sc[1], sc[2]
    q_inv = [sc[3], sc[4], sc[5]]
    rest = [sc[6], sc[7], sc[8]]
    keep = [sc[9], sc[10], sc[11]]
    gain = [sc[12], sc[13], sc[14]]
    h0, h1 = sc[15], sc[16]
    h0_a, h0_b, h1_b, h1_c = sc[17], sc[18], sc[19], sc[20]
    back = sc[21]
    pull = sc[22]

    def teacher(state, level, first):
        last = total - first
        conv1(state, q_inv[level], t_w1, first, last, 8, False)
        conv2(t_w2, t_pr, first + 1, last - 1, 6, False)

    def update(dst, first, fn):
        def body(r):
            at = pl.ds(r, 2)
            dst[at] = fn(at)

        blocks(first, total - first, 2, body)

    def euler(src, dst, first, level, ratio):
        cx = jnp.where(is_x, 1.0 + ratio * rest[level], 1.0)
        cf = ratio * gain[level]
        update(dst, first, lambda at: src[at] * cx - fld[at] * cf)

    def correct(src, guess, dst, first, level, ratio):
        cx = jnp.where(is_x, 0.5 + 0.5 * ratio * rest[level], 0.5)
        cf = 0.5 * ratio * gain[level]
        update(dst, first, lambda at: 0.5 * src[at] + guess[at] * cx - fld[at] * cf)

    teacher(x0, 0, 1)
    euler(x0, xa, 2, 0, h0_a)
    teacher(xa, 1, 3)
    correct(x0, xa, xb, 4, 1, h0_b)
    teacher(xb, 1, 5)
    euler(xb, xa, 6, 1, h1_b)
    teacher(xa, 2, 7)
    correct(xb, xa, xb, 8, 2, h1_c)

    def make_target(at):
        start = x0[at]
        return start - (xb[at] - start) * back

    update(xa, 8, make_target)

    for first in range(0, rows, 16):
        count = min(16, rows - first)
        even = jnp.zeros((center, 128), F32)
        odd = even
        group = lax.broadcasted_iota(jnp.int32, (center, 128), 1) // 8
        for i in range(count):
            row = xa[HALO + first + i, 0:center]
            even = jnp.where(group == i, pltpu.roll(row, (8 * i + 120) % 128, 1), even)
            odd = jnp.where(group == i, pltpu.roll(row, (8 * i + 112) % 128, 1), odd)
        turned[pl.ds(0, center, stride=2)] = even
        turned[pl.ds(1, center, stride=2)] = odd
        flat = turned[0:cols].T
        for i in range(count):
            tgt_ref[:, first + i, :] = flat[8 * i : 8 * i + 4]

    conv1(x0, q_inv[0], s_w1, 7, total - 7, 4, True)
    conv2(s_w2, s_pr, 8, total - 8, 6, True)

    def backward(r):
        at = pl.ds(r, 2)
        d_field = jnp.where(
            is_x, pull * (keep[0] * x0[at] + gain[0] * fld[at] - xa[at]), 0.0
        ).astype(BF16)
        d_gated = jnp.dot(
            d_field.reshape(2 * pairs, 128), s_pt[...], preferred_element_type=F32
        ).reshape(2, pairs, 256)
        spread(d_gated * slope2[at], dz4, r, 2)

    blocks(8, total - 8, 2, backward)
    zero_edges(dz4)

    cells = rows * center
    dims = (((0,), (0,)), ((), ()))
    middle = pl.ds(HALO, rows)
    dz = dz4[middle, 0:center, 128:384].reshape(cells, 256)
    for a in range(3):
        near = x4[pl.ds(HALO - 1 + a, rows), 0:center, :].reshape(cells, 512)
        grad = lax.dot_general(dz, near, dims, preferred_element_type=F32)
        for b in range(3):
            at = (3 * a + b) * C
            sum_a[at : at + C] = (
                grad[:128, b * C : (b + 1) * C] + grad[128:, (b + 1) * C : (b + 2) * C]
            )
    if plane * chunk_a > 9 * C:
        sum_a[9 * C :] = jnp.zeros((plane * chunk_a - 9 * C, C), F32)
        sum_b[C:] = jnp.zeros((plane * chunk_b - C, C), F32)
    for n in range(plane):
        out_a[n] = sum_a[n * chunk_a : (n + 1) * chunk_a].astype(BF16)
    scatter_a = exchange(plane, in_plane, lambda o: out_a.at[o], lambda step: in_a.at[step - 1])

    def conv3(r):
        lhs = jnp.concatenate(
            [dz4[pl.ds(r + a - 1, 4)].reshape(4 * pairs, 512) for a in range(3)], axis=1
        )
        dh = jnp.dot(lhs, s_r[...], preferred_element_type=F32).reshape(4, pairs, 256)
        dpre[pl.ds(r - HALO, 4)] = (dh * slope1[pl.ds(r, 4)]).astype(BF16)

    blocks(HALO, HALO + rows, 4, conv3)
    d_before = dpre[:, 0:center, :].reshape(cells, 256)
    near = u2[middle, 0:center, :].reshape(cells, 128)
    grad = lax.dot_general(d_before, near, dims, preferred_element_type=F32)
    sum_b[0:C] = grad[:128] + pltpu.roll(grad[128:], 120, 1)
    for n in range(plane):
        out_b[n] = sum_b[n * chunk_b : (n + 1) * chunk_b].astype(BF16)
    scatter_b = exchange(plane, in_plane, lambda o: out_b.at[o], lambda step: in_b.at[step - 1])

    for copy in scatter_a:
        copy.wait()
    own_a = sum_a[pl.ds(pl.multiple_of(spot * chunk_a, 8), chunk_a)]
    for n in range(plane - 1):
        own_a = own_a + in_a[n].astype(F32)
    for copy in scatter_b:
        copy.wait()
    own_b = sum_b[pl.ds(pl.multiple_of(spot * chunk_b, 8), chunk_b)]
    for n in range(plane - 1):
        own_b = own_b + in_b[n].astype(F32)
    own = jnp.concatenate([own_a, own_b], axis=0)
    for n in range(depth):
        held[n] = own[n * piece : (n + 1) * piece]
    for copy in exchange(
        depth, in_line, lambda o: held.at[o], lambda step: line_in.at[step - 1]
    ):
        copy.wait()
    whole = held[line]
    for n in range(depth - 1):
        whole = whole + line_in[n]
    line_all[line] = whole
    for copy in exchange(
        depth, in_line, lambda o: line_all.at[line], lambda step: line_all.at[line]
    ):
        copy.wait()
    plane_all[spot] = line_all[...].reshape(chunk, 128).astype(BF16)
    for copy in exchange(
        plane, in_plane, lambda o: plane_all.at[spot], lambda step: plane_all.at[spot]
    ):
        copy.wait()

    size = 1.0 / (9 * C * C)
    both = plane_all[:, 0:chunk_a].reshape(plane * chunk_a, 128).astype(F32)
    spots = plane_all[:, chunk_a:chunk].reshape(plane * chunk_b, 128).astype(F32)[0:C]
    second = [both[t * C : (t + 1) * C] for t in range(9)]
    tall = jnp.concatenate([s_lift[...].astype(F32)] * 16, axis=0)
    group = lax.broadcasted_iota(jnp.int32, (128, 128), 0) // 8
    first = [
        jnp.dot(
            spots,
            jnp.where(group == 4 * (t // 3) + t % 3, tall, 0.0),
            precision=lax.Precision.HIGHEST,
            preferred_element_type=F32,
        )
        for t in range(9)
    ]
    for parts, ref in ((first, first_ref), (second, second_ref)):
        squares = parts[0] * parts[0]
        for t in range(1, 9):
            squares = squares + parts[t] * parts[t]
        factor = lax.rsqrt(jnp.sum(squares, keepdims=True) * size + 1e-06)
        for t in range(9):
            ref[t] = parts[t] * factor


def local(
    clean, noise, mean_field, sigma_index,
    teacher_lift, teacher_first, teacher_second, teacher_proj,
    student_lift, student_first, student_second, student_proj,
):
    rows, cols = clean.shape[1:]
    lat_n, lon_n = lax.axis_size("lat"), lax.axis_size("lon")
    total, pairs, center = rows + 2 * HALO, (cols + 2 * SIDE) // 2, cols // 2
    vmem = pl.BlockSpec(memory_space=pltpu.VMEM)
    smem = pl.BlockSpec(memory_space=pltpu.SMEM)
    table = jnp.asarray(scalar_table().reshape(-1))

    offsets = [0, 1] if lon_n == 2 else [0, 1, -1]
    slots = len(offsets)
    inner = 4 if lat_n % 4 == 0 else 1
    depth, plane = lat_n // inner, inner * lon_n
    chunk_a = -(-9 * C // (plane * 16)) * 16
    chunk_b = -(-C // (plane * 16)) * 16
    while (chunk_a + chunk_b) % (8 * depth):
        chunk_b += 16
    chunk = chunk_a + chunk_b
    piece = chunk // depth
    links = 3 * slots - 1 + 3 * (plane - 1) + 2 * (depth - 1)
    target, first, second = pl.pallas_call(
        functools.partial(
            kernel, rows, pairs, center, lat_n, lon_n, offsets, inner, chunk_a, chunk_b
        ),
        out_shape=[
            jax.ShapeDtypeStruct((4, rows, cols), F32),
            jax.ShapeDtypeStruct((9, C, C), F32),
            jax.ShapeDtypeStruct((9, C, C), F32),
        ],
        in_specs=[smem, smem] + [vmem] * 11,
        out_specs=[vmem] * 3,
        scratch_shapes=[pltpu.VMEM((total, pairs, 128), F32)] * 4
        + [
            pltpu.VMEM((total, pairs, 128), BF16),
            pltpu.VMEM((total, pairs, 512), BF16),
            pltpu.VMEM((total, pairs, 512), BF16),
            pltpu.VMEM((total, pairs, 256), F32),
            pltpu.VMEM((total, pairs, 256), F32),
            pltpu.VMEM((rows, pairs, 256), BF16),
        ]
        + [
            pltpu.VMEM((2 * C, 2 * C), BF16),
            pltpu.VMEM((13 * C, 2 * C), BF16),
            pltpu.VMEM((2 * C, C), BF16),
        ]
        * 2
        + [
            pltpu.VMEM((12 * C, 2 * C), BF16),
            pltpu.VMEM((C, 2 * C), BF16),
            pltpu.VMEM((C, 2 * C), F32),
            pltpu.VMEM((2 * pairs, 128), F32),
            pltpu.VMEM((3, slots, 8, rows, cols), F32),
            pltpu.VMEM((plane * chunk_a, 128), F32),
            pltpu.VMEM((plane * chunk_b, 128), F32),
            pltpu.VMEM((plane, chunk_a, 128), BF16),
            pltpu.VMEM((plane, chunk_b, 128), BF16),
            pltpu.VMEM((plane - 1, chunk_a, 128), BF16),
            pltpu.VMEM((plane - 1, chunk_b, 128), BF16),
            pltpu.VMEM((depth, piece, 128), F32),
            pltpu.VMEM((depth - 1, piece, 128), F32),
            pltpu.VMEM((depth, piece, 128), F32),
            pltpu.VMEM((plane, chunk, 128), BF16),
            pltpu.SemaphoreType.DMA((links,)),
            pltpu.SemaphoreType.DMA((links,)),
        ],
        compiler_params=pltpu.CompilerParams(
            collective_id=0, has_side_effects=True, vmem_limit_bytes=56 * 1024 * 1024
        ),
    )(
        table, sigma_index, clean, noise, mean_field,
        *(
            taps.transpose(1, 0, 2)
            for taps in (teacher_first, teacher_second, student_first, student_second)
        ),
        teacher_lift.T, student_lift.T, teacher_proj, student_proj,
    )
    return (target, first.transpose(1, 0, 2), second.transpose(1, 0, 2))


def solution(mesh):
    grid = P(None, "lat", "lon")
    return jax.shard_map(
        local,
        mesh=mesh,
        in_specs=(grid, grid, grid) + (P(),) * 9,
        out_specs=(grid, P(), P()),
        check_vma=False,
    )
```

```python
import functools

import jax
import jax.numpy as jnp
import numpy as np
from jax import lax
from jax.experimental import pallas as pl
from jax.experimental.pallas import tpu as pltpu
from jax.sharding import PartitionSpec as P

SCHED = 18
HALO = 9
SIDE = 16
C = 128
F32 = jnp.float32
BF16 = jnp.bfloat16


def scalar_table():
    ramp = np.arange(SCHED, dtype=np.float64) / (SCHED - 1)
    top, bottom = 80.0 ** (1.0 / 7.0), 0.02 ** (1.0 / 7.0)
    sigma = (top + ramp * (bottom - top)) ** 7.0
    rows = []
    for n in range(SCHED - 2):
        sig = sigma[n : n + 3]
        s0, s1, s2 = sig
        q2 = sig * sig + 0.25
        q = np.sqrt(q2)
        lam = q2[0] / (s0 * s0 * 0.25)
        h0, h1 = s1 - s0, s2 - s1
        rows.append(
            [*sig, *(1.0 / q), *(sig * sig / q2), *(0.25 / q2), *(sig * 0.5 / q)]
            + [h0, h1, h0 / s0, h0 / s1, h1 / s1, h1 / s2, s0 / (s2 - s0)]
            + [s0 * 0.5 / q[0] * 2.0 * lam]
        )
    return np.asarray(rows, np.float32)


N_SCALARS = 23
MESH = pl.DeviceIdType.MESH


def even_block(count, largest):
    return max(n for n in range(1, largest + 1) if count % n == 0)


def silu(v):
    u = 0.5 * v
    return u + u * jnp.tanh(u)


def silu_slope(v):
    sig = 0.5 + 0.5 * jnp.tanh(0.5 * v)
    return sig * (1.0 + v * (1.0 - sig))


def kernel(
    rows, pairs, center, lat_n, lon_n, offsets, inner, chunk_a, chunk_b,
    table, index, clean, noise, mean, t_first, t_second, s_first, s_second,
    t_lift, s_lift, t_proj, s_proj,
    tgt_ref, first_ref, second_ref,
    x0, xa, xb, fld, u2, x4, dz4, slope1, slope2, dpre,
    t_w1, t_w2, t_pr, s_w1, s_w2, s_pr, s_r, s_pt, joined, turned,
    blocks_in, sum_a, sum_b, out_a, out_b, in_a, in_b, held, line_in, line_all, plane_all,
    send, recv,
):
    total = rows + 2 * HALO
    y, x = lax.axis_index("lat"), lax.axis_index("lon")
    top = y == 0
    bottom = y == lat_n - 1
    depth, plane = lat_n // inner, inner * lon_n
    chunk = chunk_a + chunk_b
    piece = chunk // depth
    line = lax.div(y, inner)
    spot = lax.rem(y, inner) * lon_n + x
    beside = []
    for dy in (0, 1, -1):
        for dx in offsets:
            if dy or dx:
                slot = [(-dx - other) % lon_n for other in offsets].index(0)
                device = (lax.rem(y + dy + lat_n, lat_n), lax.rem(x + dx + lon_n, lon_n))
                beside.append((device, 1 - dy, slot))

    def in_plane(step):
        other = lax.rem(spot + step, plane)
        return other, (line * inner + lax.div(other, lon_n), lax.rem(other, lon_n))

    def in_line(step):
        other = lax.rem(line + step, depth)
        return other, (other * inner + lax.rem(y, inner), x)

    greeted = [device for device, _, _ in beside]
    greeted += [in_plane(step)[1] for step in range(1, plane)]
    greeted += [in_line(step)[1] for step in range(1, depth)]
    barrier = pltpu.get_barrier_semaphore()
    for device in greeted:
        pl.semaphore_signal(barrier, inc=1, device_id=device, device_id_type=MESH)
    used = [0]

    def push(source, target, device):
        k = used[0]
        used[0] += 1
        copy = pltpu.make_async_remote_copy(
            src_ref=source, dst_ref=target, send_sem=send.at[k], recv_sem=recv.at[k],
            device_id=device, device_id_type=MESH,
        )
        copy.start()
        return copy

    def exchange(count, where, source, target):
        copies = []
        for step in range(1, count):
            other, device = where(step)
            copies.append(push(source(other), target(step), device))
        return copies

    base = index[0] * N_SCALARS
    sc = [table[base + k] for k in range(N_SCALARS)]
    blocks_in[1, 0, 0:4] = clean[...] + sc[0] * noise[...]
    blocks_in[1, 0, 4:8] = mean[...]
    pl.semaphore_wait(barrier, len(greeted))
    halos = [push(blocks_in.at[1, 0], blocks_in.at[sy, sx], device) for device, sy, sx in beside]
    lane = lax.broadcasted_iota(jnp.int32, (1, 1, 128), 2)
    lane_a = lane // 32
    lane_j = lane % 32 // 8
    is_x = lane % 8 < 4

    def zero_edges(ref):
        @pl.when(top)
        def _():
            ref[0:HALO] = jnp.zeros((HALO,) + ref.shape[1:], ref.dtype)

        @pl.when(bottom)
        def _():
            ref[HALO + rows : total] = jnp.zeros((HALO,) + ref.shape[1:], ref.dtype)

    def blocks(first, last, size, body):
        count = -(-(last - first) // size)
        room, gaps = last - first - size, max(count - 1, 1)

        def step(i, carry):
            body(first + i * room // gaps)
            return carry

        lax.fori_loop(0, count, step, 0)

    def place(ref, t, block):
        a, b = divmod(t, 3)
        for side in range(2):
            at = (4 * a + b + side) * C
            ref[at : at + C, side * C : (side + 1) * C] = block

    for ref in (t_w2, s_w2, s_r):
        ref[...] = jnp.zeros_like(ref)
    none = jnp.zeros((8, C), BF16)
    four = jnp.zeros((4, C), F32)
    lifts = [t_lift[...], s_lift[...]]
    taps = [t_first, t_second, s_first, s_second]
    projs = [
        jnp.concatenate([ref[...].astype(F32), four], axis=0).astype(BF16)
        for ref in (t_proj, s_proj)
    ]
    for net, w1, w2, pr in ((0, t_w1, t_w2, t_pr), (1, s_w1, s_w2, s_pr)):
        joined[...] = jnp.zeros_like(joined)
        for t in range(9):
            a, b = divmod(t, 3)
            mixed = lax.dot_general(
                lifts[net], taps[2 * net][t], (((1,), (1,)), ((), ())),
                preferred_element_type=F32,
            )
            for side in range(2):
                at = a * 32 + (b + side) * 8
                joined[at : at + 8, side * C : (side + 1) * C] = mixed
            place(w2, t, taps[2 * net + 1][t].T)
        high = joined[...].astype(BF16)
        w1[0:128] = high
        w1[128:256] = (joined[...] - high.astype(F32)).astype(BF16)
        w2[12 * C + 40 : 12 * C + 56] = jnp.concatenate(
            [
                jnp.concatenate([lifts[net], none], axis=1),
                jnp.concatenate([none, lifts[net]], axis=1),
            ],
            axis=0,
        )
        flat_lane = lax.broadcasted_iota(jnp.int32, (128, 128), 1)
        flat_row = lax.broadcasted_iota(jnp.int32, (8, 128), 0)
        flat_col = lax.broadcasted_iota(jnp.int32, (8, 128), 1)
        pick = jnp.where((flat_col % 8 == flat_row) & (flat_row < 4), 1.0, 0.0).astype(BF16)
        wide = lax.dot_general(
            projs[net], pick, (((0,), (0,)), ((), ())), preferred_element_type=F32
        )
        slot = flat_lane % 32 // 8
        odd_slot = (slot == 0) | (slot == 2)
        inside = flat_lane < 96
        pr[0:C] = jnp.where(inside & jnp.logical_not(odd_slot), wide, 0.0).astype(BF16)
        pr[C : 2 * C] = jnp.where(inside & odd_slot, wide, 0.0).astype(BF16)
    for t in range(9):
        place(s_r, t, taps[3][8 - t])
    s_pt[...] = jnp.zeros_like(s_pt)
    s_pt[40:56] = jnp.concatenate(
        [
            jnp.concatenate([projs[1], none], axis=1),
            jnp.concatenate([none, projs[1]], axis=1),
        ],
        axis=0,
    )

    cols = 2 * center
    odd_lane = (lane_j[0] == 0) | (lane_j[0] == 2)
    last_slot = blocks_in.shape[1] - 1
    column = lax.broadcasted_iota(jnp.int32, (8, cols), 1)

    def load_rows(slot, source, first, count):
        def step(i, carry):
            own = blocks_in[slot, 0, :, source + i, :]
            sides = jnp.where(
                column < SIDE,
                blocks_in[slot, 1, :, source + i, :],
                blocks_in[slot, last_slot, :, source + i, :],
            )
            turned[0:cols] = jnp.concatenate([own] * 16, axis=0).T
            sides = jnp.concatenate([sides] * 16, axis=0).T
            turned[cols : cols + SIDE] = sides[:SIDE]
            turned[cols + SIDE : cols + 2 * SIDE] = sides[cols - SIDE :]
            even = turned[pl.ds(0, pairs, stride=2)]
            odd = turned[pl.ds(1, pairs, stride=2)]
            x0[first + i] = jnp.where(odd_lane, odd, even)
            return carry

        lax.fori_loop(0, count, step, 0)

    slots = len(offsets)
    for copy in halos[: slots - 1]:
        copy.wait()
    load_rows(1, 0, HALO, rows)
    for copy in halos[slots - 1 : 2 * slots - 1]:
        copy.wait()
    load_rows(0, rows - HALO, 0, HALO)
    for copy in halos[2 * slots - 1 :]:
        copy.wait()
    load_rows(2, 0, HALO + rows, HALO)
    zero_edges(x0)

    def spread(value, ref, r, nb):
        for n in range(nb):
            row = value[n]
            ref[r + n, :, 0:128] = pltpu.roll(row[:, 128:], 1, 0).astype(BF16)
            ref[r + n, :, 128:384] = row.astype(BF16)
            ref[r + n, :, 384:512] = pltpu.roll(row[:, :128], pairs - 1, 0).astype(BF16)

    def conv1(state, q_inv, w1, first, last, nb, save):
        scale = jnp.where(is_x, q_inv, 1.0)

        def body(r):
            xs = state[pl.ds(r - 1, nb + 2)] * scale
            shifted = []
            for n in range(nb + 2):
                row = xs[n]
                back = pltpu.roll(row, 1, 0)
                ahead = pltpu.roll(row, pairs - 1, 0)
                shifted.append(jnp.where(lane_j[0] == 0, back, jnp.where(lane_j[0] == 3, ahead, row)))
            u = jnp.stack(
                [
                    jnp.where(
                        lane_a[0] == 0,
                        shifted[n],
                        jnp.where(lane_a[0] == 1, shifted[n + 1], shifted[n + 2]),
                    )
                    for n in range(nb)
                ]
            ).astype(BF16)
            u2[pl.ds(r, nb)] = u
            flat = u.reshape(nb * pairs, 128)
            pre = jnp.dot(
                jnp.concatenate([flat, flat], axis=1), w1[...], preferred_element_type=F32
            ).reshape(nb, pairs, 256)
            spread(silu(pre), x4, r, nb)
            if save:
                slope1[pl.ds(r, nb)] = silu_slope(pre)

        blocks(first, last, nb, body)
        zero_edges(x4)

    def conv2(w2, pr, first, last, nb, save):
        def body(r):
            lhs = jnp.concatenate(
                [x4[pl.ds(r + a - 1, nb)].reshape(nb * pairs, 512) for a in range(3)]
                + [u2[pl.ds(r, nb)].reshape(nb * pairs, 128)],
                axis=1,
            )
            z = jnp.dot(lhs, w2[...], preferred_element_type=F32)
            g = silu(z).astype(BF16)
            fld[pl.ds(r, nb)] = jnp.dot(g, pr[...], preferred_element_type=F32).reshape(
                nb, pairs, 128
            )
            if save:
                slope2[pl.ds(r, nb)] = silu_slope(z).reshape(nb, pairs, 256)

        blocks(first, last, nb, body)
        zero_edges(fld)

    s0, s1, s2 = sc[0], sc[1], sc[2]
    q_inv = [sc[3], sc[4], sc[5]]
    rest = [sc[6], sc[7], sc[8]]
    keep = [sc[9], sc[10], sc[11]]
    gain = [sc[12], sc[13], sc[14]]
    h0, h1 = sc[15], sc[16]
    h0_a, h0_b, h1_b, h1_c = sc[17], sc[18], sc[19], sc[20]
    back = sc[21]
    pull = sc[22]

    def teacher(state, level, first):
        last = total - first
        conv1(state, q_inv[level], t_w1, first, last, even_block(last - first, 10), False)
        conv2(t_w2, t_pr, first + 1, last - 1, even_block(last - first - 2, 13), False)

    def update(dst, first, fn):
        size = even_block(total - 2 * first, 6)

        def body(r):
            at = pl.ds(r, size)
            dst[at] = fn(at)

        blocks(first, total - first, size, body)

    def euler(src, dst, first, level, ratio):
        cx = jnp.where(is_x, 1.0 + ratio * rest[level], 1.0)
        cf = ratio * gain[level]
        update(dst, first, lambda at: src[at] * cx - fld[at] * cf)

    def correct(src, guess, dst, first, level, ratio):
        cx = jnp.where(is_x, 0.5 + 0.5 * ratio * rest[level], 0.5)
        cf = 0.5 * ratio * gain[level]
        update(dst, first, lambda at: 0.5 * src[at] + guess[at] * cx - fld[at] * cf)

    teacher(x0, 0, 1)
    euler(x0, xa, 2, 0, h0_a)
    teacher(xa, 1, 3)
    correct(x0, xa, xb, 4, 1, h0_b)
    teacher(xb, 1, 5)
    euler(xb, xa, 6, 1, h1_b)
    teacher(xa, 2, 7)
    correct(xb, xa, xb, 8, 2, h1_c)

    def make_target(at):
        start = x0[at]
        return start - (xb[at] - start) * back

    update(xa, 8, make_target)

    for first in range(0, rows, 16):
        count = min(16, rows - first)
        even = jnp.zeros((center, 128), F32)
        odd = even
        group = lax.broadcasted_iota(jnp.int32, (center, 128), 1) // 8
        for i in range(count):
            row = xa[HALO + first + i, 0:center]
            even = jnp.where(group == i, pltpu.roll(row, (8 * i + 120) % 128, 1), even)
            odd = jnp.where(group == i, pltpu.roll(row, (8 * i + 112) % 128, 1), odd)
        turned[pl.ds(0, center, stride=2)] = even
        turned[pl.ds(1, center, stride=2)] = odd
        flat = turned[0:cols].T
        for i in range(count):
            tgt_ref[:, first + i, :] = flat[8 * i : 8 * i + 4]

    conv1(x0, q_inv[0], s_w1, 7, total - 7, even_block(total - 14, 5), True)
    conv2(s_w2, s_pr, 8, total - 8, even_block(total - 16, 9), True)

    step_rows = even_block(total - 16, 6)

    def backward(r):
        at = pl.ds(r, step_rows)
        d_field = jnp.where(
            is_x, pull * (keep[0] * x0[at] + gain[0] * fld[at] - xa[at]), 0.0
        ).astype(BF16)
        d_gated = jnp.dot(
            d_field.reshape(step_rows * pairs, 128), s_pt[...], preferred_element_type=F32
        ).reshape(step_rows, pairs, 256)
        spread(d_gated * slope2[at], dz4, r, step_rows)

    blocks(8, total - 8, step_rows, backward)
    zero_edges(dz4)

    cells = rows * center
    dims = (((0,), (0,)), ((), ()))
    middle = pl.ds(HALO, rows)
    dz = dz4[middle, 0:center, 128:384].reshape(cells, 256)
    for a in range(3):
        near = x4[pl.ds(HALO - 1 + a, rows), 0:center, :].reshape(cells, 512)
        grad = lax.dot_general(dz, near, dims, preferred_element_type=F32)
        for b in range(3):
            at = (3 * a + b) * C
            sum_a[at : at + C] = (
                grad[:128, b * C : (b + 1) * C] + grad[128:, (b + 1) * C : (b + 2) * C]
            )
    if plane * chunk_a > 9 * C:
        sum_a[9 * C :] = jnp.zeros((plane * chunk_a - 9 * C, C), F32)
        sum_b[C:] = jnp.zeros((plane * chunk_b - C, C), F32)
    for n in range(plane):
        out_a[n] = sum_a[n * chunk_a : (n + 1) * chunk_a].astype(BF16)
    scatter_a = exchange(plane, in_plane, lambda o: out_a.at[o], lambda step: in_a.at[step - 1])

    conv_rows = even_block(rows, 8)

    def conv3(r):
        lhs = jnp.concatenate(
            [dz4[pl.ds(r + a - 1, conv_rows)].reshape(conv_rows * pairs, 512) for a in range(3)], axis=1
        )
        dh = jnp.dot(lhs, s_r[...], preferred_element_type=F32).reshape(
            conv_rows, pairs, 256
        )
        dpre[pl.ds(r - HALO, conv_rows)] = (dh * slope1[pl.ds(r, conv_rows)]).astype(BF16)

    blocks(HALO, HALO + rows, conv_rows, conv3)
    d_before = dpre[:, 0:center, :].reshape(cells, 256)
    near = u2[middle, 0:center, :].reshape(cells, 128)
    grad = lax.dot_general(d_before, near, dims, preferred_element_type=F32)
    sum_b[0:C] = grad[:128] + pltpu.roll(grad[128:], 120, 1)
    for n in range(plane):
        out_b[n] = sum_b[n * chunk_b : (n + 1) * chunk_b].astype(BF16)
    scatter_b = exchange(plane, in_plane, lambda o: out_b.at[o], lambda step: in_b.at[step - 1])

    for copy in scatter_a:
        copy.wait()
    own_a = sum_a[pl.ds(pl.multiple_of(spot * chunk_a, 8), chunk_a)]
    for n in range(plane - 1):
        own_a = own_a + in_a[n].astype(F32)
    for copy in scatter_b:
        copy.wait()
    own_b = sum_b[pl.ds(pl.multiple_of(spot * chunk_b, 8), chunk_b)]
    for n in range(plane - 1):
        own_b = own_b + in_b[n].astype(F32)
    own = jnp.concatenate([own_a, own_b], axis=0)
    for n in range(depth):
        held[n] = own[n * piece : (n + 1) * piece]
    for copy in exchange(
        depth, in_line, lambda o: held.at[o], lambda step: line_in.at[step - 1]
    ):
        copy.wait()
    whole = held[line]
    for n in range(depth - 1):
        whole = whole + line_in[n]
    line_all[line] = whole
    for copy in exchange(
        depth, in_line, lambda o: line_all.at[line], lambda step: line_all.at[line]
    ):
        copy.wait()
    plane_all[spot] = line_all[...].reshape(chunk, 128).astype(BF16)
    for copy in exchange(
        plane, in_plane, lambda o: plane_all.at[spot], lambda step: plane_all.at[spot]
    ):
        copy.wait()

    size = 1.0 / (9 * C * C)
    both = plane_all[:, 0:chunk_a].reshape(plane * chunk_a, 128).astype(F32)
    spots = plane_all[:, chunk_a:chunk].reshape(plane * chunk_b, 128).astype(F32)[0:C]
    second = [both[t * C : (t + 1) * C] for t in range(9)]
    tall = jnp.concatenate([s_lift[...].astype(F32)] * 16, axis=0)
    group = lax.broadcasted_iota(jnp.int32, (128, 128), 0) // 8
    first = [
        jnp.dot(
            spots,
            jnp.where(group == 4 * (t // 3) + t % 3, tall, 0.0),
            precision=lax.Precision.HIGHEST,
            preferred_element_type=F32,
        )
        for t in range(9)
    ]
    for parts, ref in ((first, first_ref), (second, second_ref)):
        squares = parts[0] * parts[0]
        for t in range(1, 9):
            squares = squares + parts[t] * parts[t]
        factor = lax.rsqrt(jnp.sum(squares, keepdims=True) * size + 1e-06)
        for t in range(9):
            ref[t] = parts[t] * factor


def local(
    clean, noise, mean_field, sigma_index,
    teacher_lift, teacher_first, teacher_second, teacher_proj,
    student_lift, student_first, student_second, student_proj,
):
    rows, cols = clean.shape[1:]
    lat_n, lon_n = lax.axis_size("lat"), lax.axis_size("lon")
    total, pairs, center = rows + 2 * HALO, (cols + 2 * SIDE) // 2, cols // 2
    vmem = pl.BlockSpec(memory_space=pltpu.VMEM)
    smem = pl.BlockSpec(memory_space=pltpu.SMEM)
    table = jnp.asarray(scalar_table().reshape(-1))

    offsets = [0, 1] if lon_n == 2 else [0, 1, -1]
    slots = len(offsets)
    inner = 4 if lat_n % 4 == 0 else 1
    depth, plane = lat_n // inner, inner * lon_n
    chunk_a = -(-9 * C // (plane * 16)) * 16
    chunk_b = -(-C // (plane * 16)) * 16
    while (chunk_a + chunk_b) % (8 * depth):
        chunk_b += 16
    chunk = chunk_a + chunk_b
    piece = chunk // depth
    links = 3 * slots - 1 + 3 * (plane - 1) + 2 * (depth - 1)
    target, first, second = pl.pallas_call(
        functools.partial(
            kernel, rows, pairs, center, lat_n, lon_n, offsets, inner, chunk_a, chunk_b
        ),
        out_shape=[
            jax.ShapeDtypeStruct((4, rows, cols), F32),
            jax.ShapeDtypeStruct((9, C, C), F32),
            jax.ShapeDtypeStruct((9, C, C), F32),
        ],
        in_specs=[smem, smem] + [vmem] * 11,
        out_specs=[vmem] * 3,
        scratch_shapes=[pltpu.VMEM((total, pairs, 128), F32)] * 4
        + [
            pltpu.VMEM((total, pairs, 128), BF16),
            pltpu.VMEM((total, pairs, 512), BF16),
            pltpu.VMEM((total, pairs, 512), BF16),
            pltpu.VMEM((total, pairs, 256), F32),
            pltpu.VMEM((total, pairs, 256), F32),
            pltpu.VMEM((rows, pairs, 256), BF16),
        ]
        + [
            pltpu.VMEM((2 * C, 2 * C), BF16),
            pltpu.VMEM((13 * C, 2 * C), BF16),
            pltpu.VMEM((2 * C, C), BF16),
        ]
        * 2
        + [
            pltpu.VMEM((12 * C, 2 * C), BF16),
            pltpu.VMEM((C, 2 * C), BF16),
            pltpu.VMEM((C, 2 * C), F32),
            pltpu.VMEM((2 * pairs, 128), F32),
            pltpu.VMEM((3, slots, 8, rows, cols), F32),
            pltpu.VMEM((plane * chunk_a, 128), F32),
            pltpu.VMEM((plane * chunk_b, 128), F32),
            pltpu.VMEM((plane, chunk_a, 128), BF16),
            pltpu.VMEM((plane, chunk_b, 128), BF16),
            pltpu.VMEM((plane - 1, chunk_a, 128), BF16),
            pltpu.VMEM((plane - 1, chunk_b, 128), BF16),
            pltpu.VMEM((depth, piece, 128), F32),
            pltpu.VMEM((depth - 1, piece, 128), F32),
            pltpu.VMEM((depth, piece, 128), F32),
            pltpu.VMEM((plane, chunk, 128), BF16),
            pltpu.SemaphoreType.DMA((links,)),
            pltpu.SemaphoreType.DMA((links,)),
        ],
        compiler_params=pltpu.CompilerParams(
            collective_id=0, has_side_effects=True, vmem_limit_bytes=56 * 1024 * 1024
        ),
    )(
        table, sigma_index, clean, noise, mean_field,
        *(
            taps.transpose(1, 0, 2)
            for taps in (teacher_first, teacher_second, student_first, student_second)
        ),
        teacher_lift.T, student_lift.T, teacher_proj, student_proj,
    )
    return (target, first.transpose(1, 0, 2), second.transpose(1, 0, 2))


def solution(mesh):
    grid = P(None, "lat", "lon")
    return jax.shard_map(
        local,
        mesh=mesh,
        in_specs=(grid, grid, grid) + (P(),) * 9,
        out_specs=(grid, P(), P()),
        check_vma=False,
    )
```

```python
import functools

import jax
import jax.numpy as jnp
import numpy as np
from jax import lax
from jax.experimental import pallas as pl
from jax.experimental.pallas import tpu as pltpu
from jax.sharding import PartitionSpec as P

SCHED = 18
HALO = 9
SIDE = 16
C = 128
F32 = jnp.float32
BF16 = jnp.bfloat16


def scalar_table():
    ramp = np.arange(SCHED, dtype=np.float64) / (SCHED - 1)
    top, bottom = 80.0 ** (1.0 / 7.0), 0.02 ** (1.0 / 7.0)
    sigma = (top + ramp * (bottom - top)) ** 7.0
    rows = []
    for n in range(SCHED - 2):
        sig = sigma[n : n + 3]
        s0, s1, s2 = sig
        q2 = sig * sig + 0.25
        q = np.sqrt(q2)
        lam = q2[0] / (s0 * s0 * 0.25)
        h0, h1 = s1 - s0, s2 - s1
        rows.append(
            [*sig, *(1.0 / q), *(sig * sig / q2), *(0.25 / q2), *(sig * 0.5 / q)]
            + [h0, h1, h0 / s0, h0 / s1, h1 / s1, h1 / s2, s0 / (s2 - s0)]
            + [s0 * 0.5 / q[0] * 2.0 * lam]
        )
    return np.asarray(rows, np.float32)


N_SCALARS = 23
MESH = pl.DeviceIdType.MESH


def even_block(count, largest):
    return max(n for n in range(1, largest + 1) if count % n == 0)


def silu(v):
    u = 0.5 * v
    return u + u * jnp.tanh(u)


def silu_slope(v):
    sig = 0.5 + 0.5 * jnp.tanh(0.5 * v)
    return sig * (1.0 + v * (1.0 - sig))


def kernel(
    rows, pairs, center, lat_n, lon_n, offsets, inner, chunk_a, chunk_b,
    table, index, clean, noise, mean, t_first, t_second, s_first, s_second,
    t_lift, s_lift, t_proj, s_proj,
    tgt_ref, first_ref, second_ref,
    x0, xa, xb, fld, u2, x4, dz4, slope1, slope2, dpre,
    t_w1, t_w2, t_pr, s_w1, s_w2, s_pr, s_r, s_pt, joined, turned,
    blocks_in, sum_a, sum_b, out_a, out_b, in_a, in_b, held, line_in, line_all, plane_all,
    send, recv,
):
    total = rows + 2 * HALO
    y, x = lax.axis_index("lat"), lax.axis_index("lon")
    top = y == 0
    bottom = y == lat_n - 1
    depth, plane = lat_n // inner, inner * lon_n
    chunk = chunk_a + chunk_b
    piece = chunk // depth
    line = lax.div(y, inner)
    spot = lax.rem(y, inner) * lon_n + x
    beside = []
    for dy in (0, 1, -1):
        for dx in offsets:
            if dy or dx:
                slot = [(-dx - other) % lon_n for other in offsets].index(0)
                device = (lax.rem(y + dy + lat_n, lat_n), lax.rem(x + dx + lon_n, lon_n))
                beside.append((device, 1 - dy, slot))

    def in_plane(step):
        other = lax.rem(spot + step, plane)
        return other, (line * inner + lax.div(other, lon_n), lax.rem(other, lon_n))

    def in_line(step):
        other = lax.rem(line + step, depth)
        return other, (other * inner + lax.rem(y, inner), x)

    greeted = [device for device, _, _ in beside]
    greeted += [in_plane(step)[1] for step in range(1, plane)]
    greeted += [in_line(step)[1] for step in range(1, depth)]
    barrier = pltpu.get_barrier_semaphore()
    for device in greeted:
        pl.semaphore_signal(barrier, inc=1, device_id=device, device_id_type=MESH)
    used = [0]

    def push(source, target, device):
        k = used[0]
        used[0] += 1
        copy = pltpu.make_async_remote_copy(
            src_ref=source, dst_ref=target, send_sem=send.at[k], recv_sem=recv.at[k],
            device_id=device, device_id_type=MESH,
        )
        copy.start()
        return copy

    def exchange(count, where, source, target):
        copies = []
        for step in range(1, count):
            other, device = where(step)
            copies.append(push(source(other), target(step), device))
        return copies

    base = index[0] * N_SCALARS
    sc = [table[base + k] for k in range(N_SCALARS)]
    blocks_in[1, 0, 0:4] = clean[...] + sc[0] * noise[...]
    blocks_in[1, 0, 4:8] = mean[...]
    pl.semaphore_wait(barrier, len(greeted))
    halos = [push(blocks_in.at[1, 0], blocks_in.at[sy, sx], device) for device, sy, sx in beside]
    lane = lax.broadcasted_iota(jnp.int32, (1, 1, 128), 2)
    lane_a = lane // 32
    lane_j = lane % 32 // 8
    is_x = lane % 8 < 4

    def zero_edges(ref):
        @pl.when(top)
        def _():
            ref[0:HALO] = jnp.zeros((HALO,) + ref.shape[1:], ref.dtype)

        @pl.when(bottom)
        def _():
            ref[HALO + rows : total] = jnp.zeros((HALO,) + ref.shape[1:], ref.dtype)

    def blocks(first, last, size, body):
        count = -(-(last - first) // size)
        room, gaps = last - first - size, max(count - 1, 1)

        def step(i, carry):
            body(first + i * room // gaps)
            return carry

        lax.fori_loop(0, count, step, 0)

    def place(ref, t, block):
        a, b = divmod(t, 3)
        for side in range(2):
            at = (4 * a + b + side) * C
            ref[at : at + C, side * C : (side + 1) * C] = block

    for ref in (t_w2, s_w2, s_r):
        ref[...] = jnp.zeros_like(ref)
    none = jnp.zeros((8, C), BF16)
    four = jnp.zeros((4, C), F32)
    lifts = [t_lift[...], s_lift[...]]
    taps = [t_first, t_second, s_first, s_second]
    projs = [
        jnp.concatenate([ref[...].astype(F32), four], axis=0).astype(BF16)
        for ref in (t_proj, s_proj)
    ]
    for net, w1, w2, pr in ((0, t_w1, t_w2, t_pr), (1, s_w1, s_w2, s_pr)):
        joined[...] = jnp.zeros_like(joined)
        for t in range(9):
            a, b = divmod(t, 3)
            mixed = lax.dot_general(
                lifts[net], taps[2 * net][t], (((1,), (1,)), ((), ())),
                preferred_element_type=F32,
            )
            for side in range(2):
                at = a * 32 + (b + side) * 8
                joined[at : at + 8, side * C : (side + 1) * C] = mixed
            place(w2, t, taps[2 * net + 1][t].T)
        high = joined[...].astype(BF16)
        w1[0:128] = high
        w1[128:256] = (joined[...] - high.astype(F32)).astype(BF16)
        w2[12 * C + 40 : 12 * C + 56] = jnp.concatenate(
            [
                jnp.concatenate([lifts[net], none], axis=1),
                jnp.concatenate([none, lifts[net]], axis=1),
            ],
            axis=0,
        )
        flat_lane = lax.broadcasted_iota(jnp.int32, (128, 128), 1)
        flat_row = lax.broadcasted_iota(jnp.int32, (8, 128), 0)
        flat_col = lax.broadcasted_iota(jnp.int32, (8, 128), 1)
        pick = jnp.where((flat_col % 8 == flat_row) & (flat_row < 4), 1.0, 0.0).astype(BF16)
        wide = lax.dot_general(
            projs[net], pick, (((0,), (0,)), ((), ())), preferred_element_type=F32
        )
        slot = flat_lane % 32 // 8
        odd_slot = (slot == 0) | (slot == 2)
        inside = flat_lane < 96
        pr[0:C] = jnp.where(inside & jnp.logical_not(odd_slot), wide, 0.0).astype(BF16)
        pr[C : 2 * C] = jnp.where(inside & odd_slot, wide, 0.0).astype(BF16)
    for t in range(9):
        place(s_r, t, taps[3][8 - t])
    s_pt[...] = jnp.zeros_like(s_pt)
    s_pt[40:56] = jnp.concatenate(
        [
            jnp.concatenate([projs[1], none], axis=1),
            jnp.concatenate([none, projs[1]], axis=1),
        ],
        axis=0,
    )

    cols = 2 * center
    odd_lane = (lane_j[0] == 0) | (lane_j[0] == 2)
    last_slot = blocks_in.shape[1] - 1
    column = lax.broadcasted_iota(jnp.int32, (8, cols), 1)

    def load_rows(slot, source, first, count):
        def step(i, carry):
            own = blocks_in[slot, 0, :, source + i, :]
            sides = jnp.where(
                column < SIDE,
                blocks_in[slot, 1, :, source + i, :],
                blocks_in[slot, last_slot, :, source + i, :],
            )
            turned[0:cols] = jnp.concatenate([own] * 16, axis=0).T
            sides = jnp.concatenate([sides] * 16, axis=0).T
            turned[cols : cols + SIDE] = sides[:SIDE]
            turned[cols + SIDE : cols + 2 * SIDE] = sides[cols - SIDE :]
            even = turned[pl.ds(0, pairs, stride=2)]
            odd = turned[pl.ds(1, pairs, stride=2)]
            x0[first + i] = jnp.where(odd_lane, odd, even)
            return carry

        lax.fori_loop(0, count, step, 0)

    slots = len(offsets)
    for copy in halos[: slots - 1]:
        copy.wait()
    load_rows(1, 0, HALO, rows)
    for copy in halos[slots - 1 : 2 * slots - 1]:
        copy.wait()
    load_rows(0, rows - HALO, 0, HALO)
    for copy in halos[2 * slots - 1 :]:
        copy.wait()
    load_rows(2, 0, HALO + rows, HALO)
    zero_edges(x0)

    def spread(value, ref, r, nb):
        for n in range(nb):
            row = value[n]
            ref[r + n, :, 0:128] = pltpu.roll(row[:, 128:], 1, 0).astype(BF16)
            ref[r + n, :, 128:384] = row.astype(BF16)
            ref[r + n, :, 384:512] = pltpu.roll(row[:, :128], pairs - 1, 0).astype(BF16)

    def conv1(state, q_inv, w1, first, last, nb, save):
        scale = jnp.where(is_x, q_inv, 1.0)

        def body(r):
            xs = state[pl.ds(r - 1, nb + 2)] * scale
            shifted = []
            for n in range(nb + 2):
                row = xs[n]
                back = pltpu.roll(row, 1, 0)
                ahead = pltpu.roll(row, pairs - 1, 0)
                shifted.append(jnp.where(lane_j[0] == 0, back, jnp.where(lane_j[0] == 3, ahead, row)))
            u = jnp.stack(
                [
                    jnp.where(
                        lane_a[0] == 0,
                        shifted[n],
                        jnp.where(lane_a[0] == 1, shifted[n + 1], shifted[n + 2]),
                    )
                    for n in range(nb)
                ]
            ).astype(BF16)
            u2[pl.ds(r, nb)] = u
            flat = u.reshape(nb * pairs, 128)
            pre = jnp.dot(
                jnp.concatenate([flat, flat], axis=1), w1[...], preferred_element_type=F32
            ).reshape(nb, pairs, 256)
            spread(silu(pre), x4, r, nb)
            if save:
                slope1[pl.ds(r, nb)] = silu_slope(pre)

        blocks(first, last, nb, body)
        zero_edges(x4)

    def conv2(w2, pr, first, last, nb, save):
        def body(r):
            lhs = jnp.concatenate(
                [x4[pl.ds(r + a - 1, nb)].reshape(nb * pairs, 512) for a in range(3)]
                + [u2[pl.ds(r, nb)].reshape(nb * pairs, 128)],
                axis=1,
            )
            z = jnp.dot(lhs, w2[...], preferred_element_type=F32)
            g = silu(z).astype(BF16)
            fld[pl.ds(r, nb)] = jnp.dot(g, pr[...], preferred_element_type=F32).reshape(
                nb, pairs, 128
            )
            if save:
                slope2[pl.ds(r, nb)] = silu_slope(z).reshape(nb, pairs, 256)

        blocks(first, last, nb, body)
        zero_edges(fld)

    s0, s1, s2 = sc[0], sc[1], sc[2]
    q_inv = [sc[3], sc[4], sc[5]]
    rest = [sc[6], sc[7], sc[8]]
    keep = [sc[9], sc[10], sc[11]]
    gain = [sc[12], sc[13], sc[14]]
    h0, h1 = sc[15], sc[16]
    h0_a, h0_b, h1_b, h1_c = sc[17], sc[18], sc[19], sc[20]
    back = sc[21]
    pull = sc[22]

    def teacher(state, level, first):
        last = total - first
        conv1(state, q_inv[level], t_w1, first, last, even_block(last - first, 16), False)
        conv2(t_w2, t_pr, first + 1, last - 1, even_block(last - first - 2, 15), False)

    def update(dst, first, fn):
        size = even_block(total - 2 * first, 10)

        def body(r):
            at = pl.ds(r, size)
            dst[at] = fn(at)

        blocks(first, total - first, size, body)

    def euler(src, dst, first, level, ratio):
        cx = jnp.where(is_x, 1.0 + ratio * rest[level], 1.0)
        cf = ratio * gain[level]
        update(dst, first, lambda at: src[at] * cx - fld[at] * cf)

    def correct(src, guess, dst, first, level, ratio):
        cx = jnp.where(is_x, 0.5 + 0.5 * ratio * rest[level], 0.5)
        cf = 0.5 * ratio * gain[level]
        update(dst, first, lambda at: 0.5 * src[at] + guess[at] * cx - fld[at] * cf)

    teacher(x0, 0, 1)
    euler(x0, xa, 2, 0, h0_a)
    teacher(xa, 1, 3)
    correct(x0, xa, xb, 4, 1, h0_b)
    teacher(xb, 1, 5)
    euler(xb, xa, 6, 1, h1_b)
    teacher(xa, 2, 7)
    correct(xb, xa, xb, 8, 2, h1_c)

    def make_target(at):
        start = x0[at]
        return start - (xb[at] - start) * back

    update(xa, 8, make_target)

    for first in range(0, rows, 16):
        count = min(16, rows - first)
        even = jnp.zeros((center, 128), F32)
        odd = even
        group = lax.broadcasted_iota(jnp.int32, (center, 128), 1) // 8
        for i in range(count):
            row = xa[HALO + first + i, 0:center]
            even = jnp.where(group == i, pltpu.roll(row, (8 * i + 120) % 128, 1), even)
            odd = jnp.where(group == i, pltpu.roll(row, (8 * i + 112) % 128, 1), odd)
        turned[pl.ds(0, center, stride=2)] = even
        turned[pl.ds(1, center, stride=2)] = odd
        flat = turned[0:cols].T
        for i in range(count):
            tgt_ref[:, first + i, :] = flat[8 * i : 8 * i + 4]

    conv1(x0, q_inv[0], s_w1, 7, total - 7, even_block(total - 14, 10), True)
    conv2(s_w2, s_pr, 8, total - 8, even_block(total - 16, 9), True)

    step_rows = even_block(total - 16, 9)

    def backward(r):
        at = pl.ds(r, step_rows)
        d_field = jnp.where(
            is_x, pull * (keep[0] * x0[at] + gain[0] * fld[at] - xa[at]), 0.0
        ).astype(BF16)
        d_gated = jnp.dot(
            d_field.reshape(step_rows * pairs, 128), s_pt[...], preferred_element_type=F32
        ).reshape(step_rows, pairs, 256)
        spread(d_gated * slope2[at], dz4, r, step_rows)

    blocks(8, total - 8, step_rows, backward)
    zero_edges(dz4)

    cells = rows * center
    dims = (((0,), (0,)), ((), ()))
    middle = pl.ds(HALO, rows)
    dz = dz4[middle, 0:center, 128:384].reshape(cells, 256)
    for a in range(3):
        near = x4[pl.ds(HALO - 1 + a, rows), 0:center, :].reshape(cells, 512)
        grad = lax.dot_general(dz, near, dims, preferred_element_type=F32)
        for b in range(3):
            at = (3 * a + b) * C
            sum_a[at : at + C] = (
                grad[:128, b * C : (b + 1) * C] + grad[128:, (b + 1) * C : (b + 2) * C]
            )
    if plane * chunk_a > 9 * C:
        sum_a[9 * C :] = jnp.zeros((plane * chunk_a - 9 * C, C), F32)
        sum_b[C:] = jnp.zeros((plane * chunk_b - C, C), F32)
    for n in range(plane):
        out_a[n] = sum_a[n * chunk_a : (n + 1) * chunk_a].astype(BF16)
    scatter_a = exchange(plane, in_plane, lambda o: out_a.at[o], lambda step: in_a.at[step - 1])

    conv_rows = even_block(rows, 16)

    def conv3(r):
        lhs = jnp.concatenate(
            [dz4[pl.ds(r + a - 1, conv_rows)].reshape(conv_rows * pairs, 512) for a in range(3)], axis=1
        )
        dh = jnp.dot(lhs, s_r[...], preferred_element_type=F32).reshape(
            conv_rows, pairs, 256
        )
        dpre[pl.ds(r - HALO, conv_rows)] = (dh * slope1[pl.ds(r, conv_rows)]).astype(BF16)

    blocks(HALO, HALO + rows, conv_rows, conv3)
    d_before = dpre[:, 0:center, :].reshape(cells, 256)
    near = u2[middle, 0:center, :].reshape(cells, 128)
    grad = lax.dot_general(d_before, near, dims, preferred_element_type=F32)
    sum_b[0:C] = grad[:128] + pltpu.roll(grad[128:], 120, 1)
    for n in range(plane):
        out_b[n] = sum_b[n * chunk_b : (n + 1) * chunk_b].astype(BF16)
    scatter_b = exchange(plane, in_plane, lambda o: out_b.at[o], lambda step: in_b.at[step - 1])

    for copy in scatter_a:
        copy.wait()
    own_a = sum_a[pl.ds(pl.multiple_of(spot * chunk_a, 8), chunk_a)]
    for n in range(plane - 1):
        own_a = own_a + in_a[n].astype(F32)
    for copy in scatter_b:
        copy.wait()
    own_b = sum_b[pl.ds(pl.multiple_of(spot * chunk_b, 8), chunk_b)]
    for n in range(plane - 1):
        own_b = own_b + in_b[n].astype(F32)
    own = jnp.concatenate([own_a, own_b], axis=0)
    for n in range(depth):
        held[n] = own[n * piece : (n + 1) * piece]
    for copy in exchange(
        depth, in_line, lambda o: held.at[o], lambda step: line_in.at[step - 1]
    ):
        copy.wait()
    whole = held[line]
    for n in range(depth - 1):
        whole = whole + line_in[n]
    line_all[line] = whole
    for copy in exchange(
        depth, in_line, lambda o: line_all.at[line], lambda step: line_all.at[line]
    ):
        copy.wait()
    plane_all[spot] = line_all[...].reshape(chunk, 128).astype(BF16)
    for copy in exchange(
        plane, in_plane, lambda o: plane_all.at[spot], lambda step: plane_all.at[spot]
    ):
        copy.wait()

    size = 1.0 / (9 * C * C)
    both = plane_all[:, 0:chunk_a].reshape(plane * chunk_a, 128).astype(F32)
    spots = plane_all[:, chunk_a:chunk].reshape(plane * chunk_b, 128).astype(F32)[0:C]
    second = [both[t * C : (t + 1) * C] for t in range(9)]
    tall = jnp.concatenate([s_lift[...].astype(F32)] * 16, axis=0)
    group = lax.broadcasted_iota(jnp.int32, (128, 128), 0) // 8
    first = [
        jnp.dot(
            spots,
            jnp.where(group == 4 * (t // 3) + t % 3, tall, 0.0),
            precision=lax.Precision.HIGHEST,
            preferred_element_type=F32,
        )
        for t in range(9)
    ]
    for parts, ref in ((first, first_ref), (second, second_ref)):
        squares = parts[0] * parts[0]
        for t in range(1, 9):
            squares = squares + parts[t] * parts[t]
        factor = lax.rsqrt(jnp.sum(squares, keepdims=True) * size + 1e-06)
        for t in range(9):
            ref[t] = parts[t] * factor


def local(
    clean, noise, mean_field, sigma_index,
    teacher_lift, teacher_first, teacher_second, teacher_proj,
    student_lift, student_first, student_second, student_proj,
):
    rows, cols = clean.shape[1:]
    lat_n, lon_n = lax.axis_size("lat"), lax.axis_size("lon")
    total, pairs, center = rows + 2 * HALO, (cols + 2 * SIDE) // 2, cols // 2
    vmem = pl.BlockSpec(memory_space=pltpu.VMEM)
    smem = pl.BlockSpec(memory_space=pltpu.SMEM)
    table = jnp.asarray(scalar_table().reshape(-1))

    offsets = [0, 1] if lon_n == 2 else [0, 1, -1]
    slots = len(offsets)
    inner = 4 if lat_n % 4 == 0 else 1
    depth, plane = lat_n // inner, inner * lon_n
    chunk_a = -(-9 * C // (plane * 16)) * 16
    chunk_b = -(-C // (plane * 16)) * 16
    while (chunk_a + chunk_b) % (8 * depth):
        chunk_b += 16
    chunk = chunk_a + chunk_b
    piece = chunk // depth
    links = 3 * slots - 1 + 3 * (plane - 1) + 2 * (depth - 1)
    target, first, second = pl.pallas_call(
        functools.partial(
            kernel, rows, pairs, center, lat_n, lon_n, offsets, inner, chunk_a, chunk_b
        ),
        out_shape=[
            jax.ShapeDtypeStruct((4, rows, cols), F32),
            jax.ShapeDtypeStruct((9, C, C), F32),
            jax.ShapeDtypeStruct((9, C, C), F32),
        ],
        in_specs=[smem, smem] + [vmem] * 11,
        out_specs=[vmem] * 3,
        scratch_shapes=[pltpu.VMEM((total, pairs, 128), F32)] * 4
        + [
            pltpu.VMEM((total, pairs, 128), BF16),
            pltpu.VMEM((total, pairs, 512), BF16),
            pltpu.VMEM((total, pairs, 512), BF16),
            pltpu.VMEM((total, pairs, 256), F32),
            pltpu.VMEM((total, pairs, 256), F32),
            pltpu.VMEM((rows, pairs, 256), BF16),
        ]
        + [
            pltpu.VMEM((2 * C, 2 * C), BF16),
            pltpu.VMEM((13 * C, 2 * C), BF16),
            pltpu.VMEM((2 * C, C), BF16),
        ]
        * 2
        + [
            pltpu.VMEM((12 * C, 2 * C), BF16),
            pltpu.VMEM((C, 2 * C), BF16),
            pltpu.VMEM((C, 2 * C), F32),
            pltpu.VMEM((2 * pairs, 128), F32),
            pltpu.VMEM((3, slots, 8, rows, cols), F32),
            pltpu.VMEM((plane * chunk_a, 128), F32),
            pltpu.VMEM((plane * chunk_b, 128), F32),
            pltpu.VMEM((plane, chunk_a, 128), BF16),
            pltpu.VMEM((plane, chunk_b, 128), BF16),
            pltpu.VMEM((plane - 1, chunk_a, 128), BF16),
            pltpu.VMEM((plane - 1, chunk_b, 128), BF16),
            pltpu.VMEM((depth, piece, 128), F32),
            pltpu.VMEM((depth - 1, piece, 128), F32),
            pltpu.VMEM((depth, piece, 128), F32),
            pltpu.VMEM((plane, chunk, 128), BF16),
            pltpu.SemaphoreType.DMA((links,)),
            pltpu.SemaphoreType.DMA((links,)),
        ],
        compiler_params=pltpu.CompilerParams(
            collective_id=0, has_side_effects=True, vmem_limit_bytes=56 * 1024 * 1024
        ),
    )(
        table, sigma_index, clean, noise, mean_field,
        *(
            taps.transpose(1, 0, 2)
            for taps in (teacher_first, teacher_second, student_first, student_second)
        ),
        teacher_lift.T, student_lift.T, teacher_proj, student_proj,
    )
    return (target, first.transpose(1, 0, 2), second.transpose(1, 0, 2))


def solution(mesh):
    grid = P(None, "lat", "lon")
    return jax.shard_map(
        local,
        mesh=mesh,
        in_specs=(grid, grid, grid) + (P(),) * 9,
        out_specs=(grid, P(), P()),
        check_vma=False,
    )
```
